32 devices in a mesh: gz: 4 (over x, core), xy: 8 (over z, y).
Axes of the slice: x: 2, y: 2, z: 4, core: 2. Of those that a mesh axis runs over, the one named last changes fastest.
Arguments:
- volume: bfloat16 [128, 64, 20480], P('gz', None, 'xy'), may hold values from -6 to 6
- occupancy: int32 [4, 160], P('gz', 'xy'), may hold values from 0 to 1, as said below
- device_order: int32 [4, 8], P('gz'), may hold values from 0 to 7, each once within a row
- weight_one: bfloat16 [64, 576], replicated, may hold values from -0.25 to 0.25
- bias_one: float32 [64], replicated, may hold values from -3 to 3
- weight_two: bfloat16 [64, 1728], replicated, may hold values from -0.15625 to 0.15625
- bias_two: float32 [64], replicated, may hold values from -3 to 3
Outputs:
- features: bfloat16 [320, 64, 512], P(('gz', 'xy'))
The draws below stay inside these ranges and needn't reach their ends.
Inputs may be any that keep to these rules, and one draw needn't show every extreme that they name: `occupancy`: each slab holds exactly 80 tissue bricks, and in each slab all 20 bricks of one xy index are tissue. `device_order`: each slab's row names every xy index once.
All inputs are finite; a program needn't handle non-finite values.
Results may differ from the reference program's by a relative error of at most 0.0025.
Values may be sent and summed in bfloat16 or wider, within the bound.
A program may use at most 256 MiB of HBM per device.

```python
import jax
import jax.numpy as jnp
from jax import lax

C = 64
BRICK = 32
XW = 4
COLS = 20
KC = 10
NZV = 128
NYX = 20480
N_GZ = 4
N_XY = 8


def draw_occupancy(key, part):
    slot_total = N_XY * COLS
    wanted_total = N_XY * KC

    def one_slab(slab_index):
        slab_key = jax.random.fold_in(jax.random.fold_in(key, 7121), slab_index)
        full_key, score_key, bias_key = jax.random.split(slab_key, 3)
        chosen = jax.random.randint(full_key, (), 0, N_XY)
        owner = jnp.arange(slot_total, dtype=jnp.int32) // COLS
        device_bias = jax.random.randint(bias_key, (N_XY,), 0, 4)
        noise = jax.random.randint(score_key, (slot_total,), 0, 4096)
        position = jnp.arange(slot_total, dtype=jnp.int32)
        score = (device_bias[owner] * 1024 + noise) * slot_total + position
        score = jnp.where(owner == chosen, 16384 * slot_total + position, score)
        ordering = jnp.argsort(-score, stable=True)
        placing = jnp.argsort(ordering, stable=True)
        return (placing < wanted_total).astype(jnp.int32)
    return jax.vmap(one_slab)(jnp.arange(N_GZ, dtype=jnp.int32))


def steps_of(key, extent, cuts, low, high):
    def one(dim, blocks):
        draws = jax.random.uniform(jax.random.fold_in(jax.random.fold_in(key, 6), dim), (blocks,), jnp.float32, low / len(cuts), high / len(cuts))
        return jnp.repeat(jnp.exp(draws), extent[dim] // blocks).reshape((-1,) + (1,) * (len(extent) - dim - 1))

    factor_of = one(*cuts[0])
    for cut in cuts[1:]:
        factor_of = factor_of * one(*cut)
    return factor_of


def gaussian(rng, dims, scale, limit, cuts=(), kind=jnp.bfloat16):
    array = jax.random.normal(rng, dims, jnp.float32) * scale
    if len(cuts) > 0:
        array = steps_of(rng, dims, cuts, -0.22, 0.18) * array
    return jnp.clip(array, min=-limit, max=limit).astype(kind)


def setup_inputs(seed: int = 0) -> dict:
    seeds = jax.random.split(jax.random.key(seed), 8)
    return {
        "volume": gaussian(seeds[0], (NZV, C, NYX), 1.0, 6.0, ((0, 4), (2, 8))),
        "occupancy": draw_occupancy(jax.random.fold_in(seeds[7], 71), 0),
        "device_order": jax.vmap(lambda own: jax.random.permutation(own, N_XY))(jax.random.split(seeds[2], N_GZ)).reshape((N_GZ, N_XY)).astype(jnp.int32),
        "weight_one": gaussian(seeds[3], (C, 9 * C), (9 * C) ** -0.5, 0.25),
        "bias_one": gaussian(seeds[4], (C,), 0.5, 3.0, (), jnp.float32),
        "weight_two": gaussian(seeds[5], (C, 27 * C), (27 * C) ** -0.5, 0.15625),
        "bias_two": gaussian(seeds[6], (C,), 0.5, 3.0, (), jnp.float32),
    }


def zone_table(length):
    position = jnp.arange(length)
    lower_end = (position == 0).astype(jnp.float32)
    upper_end = (position == length - 1).astype(jnp.float32)
    middle = 1.0 - lower_end - upper_end
    return jnp.stack([lower_end, middle, upper_end], axis=1)


def conv_chain(extended, flags, weight_one, bias_one, weight_two, bias_two):
    layers, channels, rows_ext, across = extended.shape
    inner_size = layers - 2
    moved_axes = jnp.transpose(extended, (1, 0, 2, 3))
    padded = jnp.pad(moved_axes, ((0, 0), (0, 0), (0, 0), (1, 1)))
    first_taps = [padded[:, :, row_tap:row_tap + inner_size + 2, col_tap:col_tap + across] for row_tap in range(3) for col_tap in range(3)]
    first_patches = jnp.concatenate(first_taps, axis=0).reshape(9 * channels, -1)
    first_sum = jnp.dot(weight_one, first_patches, preferred_element_type=jnp.float32)
    first_act = jax.nn.relu(first_sum + bias_one[:, None]).reshape(channels, layers, inner_size + 2, across)
    region = jnp.einsum("za,ab,yb->zy", zone_table(layers), flags.astype(jnp.float32), zone_table(inner_size + 2))
    hidden = (first_act * region[None, :, :, None]).astype(jnp.bfloat16)
    hidden_pad = jnp.pad(hidden, ((0, 0), (0, 0), (0, 0), (1, 1)))
    second_taps = [hidden_pad[:, :, row_tap:row_tap + inner_size, col_tap:col_tap + across] for row_tap in range(3) for col_tap in range(3)]
    second_patches = jnp.concatenate(second_taps, axis=0)
    second_sum = jnp.zeros((channels, inner_size * inner_size * across), jnp.float32)
    for layer_tap in range(3):
        section = second_patches[:, layer_tap:layer_tap + inner_size].reshape(9 * channels, -1)
        weights = weight_two[:, layer_tap * 9 * channels:(layer_tap + 1) * 9 * channels]
        second_sum = second_sum + jnp.dot(weights, section, preferred_element_type=jnp.float32)
    second_act = jax.nn.relu(second_sum + bias_two[:, None])
    second_act = second_act.reshape(channels, inner_size // 2, 2, inner_size // 2, 2, across // 2, 2)
    pooled = jnp.mean(second_act, axis=(2, 4, 6))
    return pooled.reshape(channels, -1).astype(jnp.bfloat16)


def neighbour_part(volume, occupancy, slab_index, column, shift_z, shift_y):
    slab_count = occupancy.shape[0]
    column_count = occupancy.shape[1]
    target_z = slab_index + shift_z
    target_y = column + shift_y
    inside = (target_z >= 0) & (target_z < slab_count) & (target_y >= 0) & (target_y < column_count)
    clip_z = jnp.clip(target_z, 0, slab_count - 1).astype(jnp.int32)
    clip_y = jnp.clip(target_y, 0, column_count - 1).astype(jnp.int32)
    present = jnp.where(inside, occupancy[clip_z, clip_y], 0)
    start_z = (clip_z * BRICK).astype(jnp.int32)
    start_y = (clip_y * (BRICK * XW)).astype(jnp.int32)
    block_data = lax.dynamic_slice(volume, (start_z, jnp.int32(0), start_y), (BRICK, C, BRICK * XW))
    block_data = block_data.reshape(BRICK, C, BRICK, XW)
    if shift_z == -1:
        block_data = block_data[BRICK - 1:]
    elif shift_z == 1:
        block_data = block_data[:1]
    if shift_y == -1:
        block_data = block_data[:, :, BRICK - 2:]
    elif shift_y == 1:
        block_data = block_data[:, :, :2]
    return block_data * present.astype(volume.dtype), present


def reference(volume, occupancy, device_order, weight_one, bias_one, weight_two, bias_two):
    ranked = jnp.argsort(1 - occupancy, axis=1, stable=True).astype(jnp.int32)
    inverse = jnp.argsort(device_order, axis=1).astype(jnp.int32)

    def one_slot(flat_index):
        slab_index = flat_index // (N_XY * KC)
        device = (flat_index // KC) % N_XY
        slot_index = flat_index % KC
        label_index = inverse[slab_index, device]
        column = ranked[slab_index, slot_index * N_XY + label_index]
        layer_rows = []
        flag_rows = []
        for shift_z in (-1, 0, 1):
            pieces = []
            marks = []
            for shift_y in (-1, 0, 1):
                piece_data, present = neighbour_part(volume, occupancy, slab_index, column, shift_z, shift_y)
                pieces.append(piece_data)
                marks.append(present.astype(jnp.float32))
            layer_rows.append(jnp.concatenate(pieces, axis=2))
            flag_rows.append(jnp.stack(marks))
        extended = jnp.concatenate(layer_rows, axis=0)
        flags = jnp.stack(flag_rows)
        return conv_chain(extended, flags, weight_one, bias_one, weight_two, bias_two)

    return lax.map(one_slot, jnp.arange(N_GZ * N_XY * KC, dtype=jnp.int32))
```

```python
import functools

import numpy as np
import jax
import jax.numpy as jnp
from jax import lax
from jax.experimental import pallas as pl
from jax.experimental.pallas import tpu as pltpu
from jax.sharding import PartitionSpec as P

BF = jnp.bfloat16
F32 = jnp.float32
SIDE = 32
ACROSS = 4
PITCH = 40


def spread_matrix():
    table = np.zeros((ACROSS * PITCH, 256), np.float32)
    for x in range(ACROSS):
        for y in range(SIDE):
            table[x * PITCH + y + 2, y * ACROSS + x] = 1
        for y in range(2):
            table[x * PITCH + 34 + y, 128 + y * ACROSS + x] = 1
            table[x * PITCH + y, 128 + (30 + y) * ACROSS + x] = 1
    return table


def interleave_matrices():
    table = np.zeros((2, 256, 512), np.float32)
    for x in range(2):
        table[x, np.arange(256), np.arange(256) * 2 + x] = 1
    return table


def banded(taps):
    zero = jnp.zeros_like(taps[..., 0, :, :])
    rows = []
    for xi in range(ACROSS):
        blocks = []
        for xo in range(ACROSS):
            tap = xi - xo + 1
            blocks.append(taps[..., tap, :, :] if 0 <= tap < 3 else zero)
        rows.append(jnp.concatenate(blocks, axis=-1))
    return jnp.concatenate(rows, axis=-2)


def brick_kernel(
    n_ref, cols_ref, slots_ref, flags_ref,
    main_ref, prev_ref, next_ref, zmain_ref, zprev_ref, znext_ref, edge_ref,
    spread_ref, inter_ref, w1_ref, b1_ref, w2_ref, b2_ref,
    out_ref,
    ext_ref, hid_ref, taps_ref, pool_ref,
    *, columns,
):
    step = pl.program_id(0)

    @pl.when(step < n_ref[0])
    def _():
        col = cols_ref[step]
        first = col == 0
        last = col == columns - 1

        def flag(a, b):
            return flags_ref[step * 9 + 3 * a + b].astype(F32)

        lane = lax.broadcasted_iota(jnp.int32, (1, 1, 128), 2)
        low = lane < 64
        from_edge = jnp.where(low, last.astype(jnp.int32), first.astype(jnp.int32)) > 0

        def rim(before, after, edge, a):
            value = jnp.where(from_edge, edge, jnp.where(low, after, before))
            mask = jnp.where(low, flag(a, 2), flag(a, 0)).astype(BF)
            return value * mask

        spread = spread_ref[...]

        def put(own, side, first_layer):
            count = own.shape[0]
            both = jnp.concatenate(
                [own.reshape(count * 64, 128), side.reshape(count * 64, 128)], axis=1
            )
            turned = lax.dot_general(
                spread, both, (((1,), (1,)), ((), ())), preferred_element_type=F32
            )
            for k in range(count):
                for half in range(2):
                    pieces = [
                        turned[x * PITCH:(x + 1) * PITCH, k * 64:(k + 1) * 64]
                        for x in (2 * half, 2 * half + 1)
                    ]
                    ext_ref[first_layer + k, 0:PITCH, half * 128:(half + 1) * 128] = (
                        jnp.concatenate(pieces, axis=1)
                    )

        def main_layers(k, carry):
            z = pl.multiple_of(k * 4, 4)
            at = pl.ds(z, 4)
            side = rim(prev_ref[at], next_ref[at], edge_ref[at], 1)
            put(main_ref[at], side, z + 1)
            return carry

        lax.fori_loop(0, 8, main_layers, 0)
        for layer, a, spot in ((0, 0, 0), (1, 2, 33)):
            at = slice(layer, layer + 1)
            side = rim(zprev_ref[at], znext_ref[at], edge_ref[32 + layer:33 + layer], a)
            put(zmain_ref[at] * flag(a, 1).astype(BF), side, spot)

        y_at = lax.broadcasted_iota(jnp.int32, (1, PITCH, 256), 1)

        def region(a):
            return jnp.where(
                y_at == 0, flag(a, 0), jnp.where(y_at == 33, flag(a, 2), flag(a, 1))
            )

        bias_one = b1_ref[...]

        def first_conv(z, count, a):
            at = pl.ds(z, count)
            rows = [
                ext_ref[at, t:t + PITCH, :].reshape(count * PITCH, 256).astype(BF)
                for t in range(3)
            ]
            total = jnp.dot(
                jnp.concatenate(rows, axis=1), w1_ref[...], preferred_element_type=F32
            )
            act = jnp.maximum(total + bias_one, 0.0).reshape(count, PITCH, 256)
            hid_ref[0:count] = act * region(a)
            for t in range(3):
                taps_ref[at, :, t * 256:(t + 1) * 256] = hid_ref[
                    0:count, t:t + SIDE, :
                ].astype(BF)

        first_conv(0, 1, 0)
        lax.fori_loop(0, 4, lambda k, c: (first_conv(k * 8 + 1, 8, 1), c)[1], 0)
        first_conv(33, 1, 2)

        bias_two = b2_ref[...]

        def second_conv(k, carry):
            z = k * 8
            total = jnp.zeros((8 * SIDE, 256), F32)
            for a in range(3):
                rows = taps_ref[pl.ds(z + a, 8)].reshape(8 * SIDE, 768)
                total = total + jnp.dot(rows, w2_ref[a], preferred_element_type=F32)
            act = jnp.maximum(total + bias_two, 0.0).reshape(4, 2, SIDE, 256)
            act = act[:, 0] + act[:, 1]
            left, right = act[..., :128], act[..., 128:]
            left = left + pltpu.roll(left, 64, 2)
            right = right + pltpu.roll(right, 64, 2)
            pool_ref[pl.ds(k * 4, 4)] = jnp.where(low, left, right)
            return carry

        lax.fori_loop(0, 4, second_conv, 0)
        pooled = pool_ref[:, pl.ds(0, 16, stride=2), :] + pool_ref[:, pl.ds(1, 16, stride=2), :]
        pooled = (pooled * 0.125).reshape(256, 128)
        turned = jnp.transpose(pooled).astype(BF)
        result = jnp.dot(turned[:64], inter_ref[0], preferred_element_type=F32)
        result = result + jnp.dot(turned[64:], inter_ref[1], preferred_element_type=F32)
        out_ref[0] = result.astype(BF)


def compute_bricks(
    count, cols, slots, flags, volume, zhalo, edge, w1, b1, w2, b2, out_slots, columns
):
    spread = jnp.asarray(spread_matrix(), BF)
    inter = jnp.asarray(interleave_matrices(), BF)

    def at(shift):
        def index(i, n, c, s, f):
            return (0, 0, jnp.clip(c[i] + shift, 0, columns - 1))
        return index

    def whole(shape):
        return pl.BlockSpec(shape, lambda i, n, c, s, f: (0,) * len(shape))

    grid_spec = pltpu.PrefetchScalarGridSpec(
        num_scalar_prefetch=4,
        grid=(columns,),
        in_specs=[pl.BlockSpec((SIDE, 64, 128), at(s)) for s in (0, -1, 1)]
        + [pl.BlockSpec((2, 64, 128), at(s)) for s in (0, -1, 1)]
        + [whole(v.shape) for v in (edge, spread, inter, w1, b1, w2, b2)],
        out_specs=pl.BlockSpec((1, 64, 512), lambda i, n, c, s, f: (s[i], 0, 0)),
        scratch_shapes=[
            pltpu.VMEM((34, 48, 256), F32),
            pltpu.VMEM((8, PITCH, 256), F32),
            pltpu.VMEM((34, SIDE, 768), BF),
            pltpu.VMEM((16, SIDE, 128), F32),
        ],
    )
    return pl.pallas_call(
        functools.partial(brick_kernel, columns=columns),
        out_shape=jax.ShapeDtypeStruct((out_slots, 64, 512), BF),
        grid_spec=grid_spec,
        compiler_params=pltpu.CompilerParams(
            dimension_semantics=("arbitrary",), vmem_limit_bytes=48 * 1024 * 1024
        ),
        cost_estimate=pl.CostEstimate(
            flops=columns * 1_600_000_000, bytes_accessed=columns * 1_600_000, transcendentals=0
        ),
    )(count, cols, slots, flags, volume, volume, volume, zhalo, zhalo, zhalo, edge,
      spread, inter, w1, b1, w2, b2)


def per_device(volume, occupancy, device_order, weight_one, bias_one, weight_two, bias_two):
    columns = occupancy.shape[1]
    slabs = lax.axis_size("gz")
    groups = lax.axis_size("xy")
    capacity = (columns + groups - 1) // groups
    slot_count = columns // 2
    me_z = lax.axis_index("gz")
    me = lax.axis_index("xy")
    rims = 2 * ACROSS

    up_z = [(i, i + 1) for i in range(slabs - 1)]
    down_z = [(j, i) for i, j in up_z]
    up_y = [(i, i + 1) for i in range(groups - 1)]
    down_y = [(j, i) for i, j in up_y]
    below = lax.ppermute(volume[SIDE - 1:], "gz", up_z)
    above = lax.ppermute(volume[:1], "gz", down_z)
    zhalo = jnp.concatenate([below, above], axis=0)
    span = volume.shape[2]
    tail = jnp.concatenate([volume[:, :, span - rims:], zhalo[:, :, span - rims:]], axis=0)
    head = jnp.concatenate([volume[:, :, :rims], zhalo[:, :, :rims]], axis=0)
    layers = tail.shape[0]
    before = lax.ppermute(tail.reshape(layers, -1), "xy", up_y).reshape(layers, 64, rims)
    after = lax.ppermute(head.reshape(layers, -1), "xy", down_y).reshape(layers, 64, rims)
    edge = jnp.concatenate(
        [after, jnp.zeros((layers, 64, 128 - 2 * rims), BF), before], axis=2
    )

    table = lax.all_gather(occupancy, ("gz", "xy"), axis=0, tiled=True)
    table = table.reshape(slabs, groups * columns)
    total = groups * columns
    marks = jnp.pad(table, ((1, 1), (1, 1)))
    near = lax.dynamic_slice(marks, (me_z, me * columns), (3, columns + 2))
    row = lax.dynamic_slice(table, (me_z, 0), (1, total))[0]
    own = occupancy[0]
    order = device_order[0]
    ids = jnp.arange(columns, dtype=jnp.int32)
    labels = jnp.arange(groups, dtype=jnp.int32)
    everyone = jnp.arange(total, dtype=jnp.int32)
    local_rank = jnp.sum(jnp.where(ids[None, :] < ids[:, None], own[None, :], 0), axis=1)
    start = jnp.sum(jnp.where(everyone < me * columns, row, 0))
    label = (start + local_rank) % groups
    target = jnp.sum(jnp.where(label[:, None] == labels[None, :], order[None, :], 0), axis=1)
    slot = target * capacity + local_rank // groups
    count = jnp.sum(own)
    wanted = jnp.minimum(ids, jnp.maximum(count - 1, 0))
    hit = (local_rank[None, :] == wanted[:, None]) & (own[None, :] > 0)
    cols = jnp.sum(jnp.where(hit, ids[None, :], 0), axis=1)
    slots = jnp.sum(jnp.where(hit, slot[None, :], 0), axis=1)
    flag_of = jnp.stack([near[a, b:b + columns] for a in range(3) for b in range(3)], axis=1)
    flags = jnp.sum(jnp.where(hit[:, :, None], flag_of[None], 0), axis=1).reshape(-1)

    w1 = banded(weight_one.reshape(64, 3, 3, 64).transpose(1, 2, 3, 0)).reshape(768, 256)
    w2 = banded(weight_two.reshape(64, 3, 3, 3, 64).transpose(1, 2, 3, 4, 0)).reshape(3, 768, 256)
    b1 = jnp.tile(bias_one, ACROSS)[None]
    b2 = jnp.tile(bias_two, ACROSS)[None]

    made = compute_bricks(
        count.reshape(1), cols, slots, flags, volume, zhalo, edge, w1, b1, w2, b2,
        groups * capacity, columns,
    )
    arrived = lax.all_to_all(made, "xy", split_axis=0, concat_axis=0, tiled=True)

    my_label = jnp.sum(jnp.where(order == me, labels, 0))
    need = jnp.arange(slot_count, dtype=jnp.int32) * groups + my_label
    counts = row.reshape(groups, columns).sum(axis=1)
    starts = jnp.sum(jnp.where(labels[None, :] < labels[:, None], counts[None, :], 0), axis=1)
    owner = jnp.sum(((starts + counts)[None, :] <= need[:, None]).astype(jnp.int32), axis=1)
    owner_start = jnp.sum(jnp.where(labels[None, :] == owner[:, None], starts[None, :], 0), axis=1)
    arrival = owner * capacity + (need - owner_start) // groups
    return jnp.take(arrived, arrival, axis=0)


def solution(mesh):
    in_specs = (P("gz", None, "xy"), P("gz", "xy"), P("gz", None), P(), P(), P(), P())
    out_specs = P(("gz", "xy"), None, None)
    return jax.shard_map(
        per_device, mesh=mesh, in_specs=in_specs, out_specs=out_specs, check_vma=False
    )
```

```python
import functools

import numpy as np
import jax
import jax.numpy as jnp
from jax import lax
from jax.experimental import pallas as pl
from jax.experimental.pallas import tpu as pltpu
from jax.sharding import PartitionSpec as P

BF = jnp.bfloat16
F32 = jnp.float32
SIDE = 32
ACROSS = 4
PITCH = 40


def spread_matrix():
    table = np.zeros((ACROSS * PITCH, 256), np.float32)
    for x in range(ACROSS):
        for y in range(SIDE):
            table[x * PITCH + y + 2, y * ACROSS + x] = 1
        for y in range(2):
            table[x * PITCH + 34 + y, 128 + y * ACROSS + x] = 1
            table[x * PITCH + y, 128 + (30 + y) * ACROSS + x] = 1
    return table


def interleave_matrices():
    table = np.zeros((2, 256, 512), np.float32)
    for x in range(2):
        table[x, np.arange(256), np.arange(256) * 2 + x] = 1
    return table


def banded(taps):
    zero = jnp.zeros_like(taps[..., 0, :, :])
    rows = []
    for xi in range(ACROSS):
        blocks = []
        for xo in range(ACROSS):
            tap = xi - xo + 1
            blocks.append(taps[..., tap, :, :] if 0 <= tap < 3 else zero)
        rows.append(jnp.concatenate(blocks, axis=-1))
    return jnp.concatenate(rows, axis=-2)


def brick_kernel(
    n_ref, cols_ref, slots_ref, flags_ref,
    main_ref, prev_ref, next_ref, zmain_ref, zprev_ref, znext_ref, edge_ref,
    spread_ref, inter_ref, w1_ref, b1_ref, w2_ref, b2_ref,
    out_ref,
    ext_ref, hid_ref, taps_ref, pool_ref,
    *, columns,
):
    step = pl.program_id(0)

    @pl.when(step < n_ref[0])
    def _():
        col = cols_ref[step]
        first = col == 0
        last = col == columns - 1

        def flag(a, b):
            return flags_ref[step * 9 + 3 * a + b].astype(F32)

        lane = lax.broadcasted_iota(jnp.int32, (1, 1, 128), 2)
        low = lane < 64
        from_edge = jnp.where(low, last.astype(jnp.int32), first.astype(jnp.int32)) > 0

        def rim(before, after, edge, a):
            value = jnp.where(from_edge, edge, jnp.where(low, after, before))
            mask = jnp.where(low, flag(a, 2), flag(a, 0)).astype(BF)
            return value * mask

        spread = spread_ref[...]

        def put(own, side, first_layer):
            count = own.shape[0]
            both = jnp.concatenate(
                [own.reshape(count * 64, 128), side.reshape(count * 64, 128)], axis=1
            )
            turned = lax.dot_general(
                spread, both, (((1,), (1,)), ((), ())), preferred_element_type=F32
            )
            for k in range(count):
                for half in range(2):
                    pieces = [
                        turned[x * PITCH:(x + 1) * PITCH, k * 64:(k + 1) * 64]
                        for x in (2 * half, 2 * half + 1)
                    ]
                    ext_ref[first_layer + k, 0:PITCH, half * 128:(half + 1) * 128] = (
                        jnp.concatenate(pieces, axis=1)
                    )

        def put_main(k):
            at = slice(4 * k, 4 * k + 4)
            put(main_ref[at], rim(prev_ref[at], next_ref[at], edge_ref[at], 1), 4 * k + 1)

        def put_rim(layer, a, spot):
            at = slice(layer, layer + 1)
            side = rim(zprev_ref[at], znext_ref[at], edge_ref[32 + layer:33 + layer], a)
            put(zmain_ref[at] * flag(a, 1).astype(BF), side, spot)

        y_at = lax.broadcasted_iota(jnp.int32, (PITCH, 256), 0)
        regions = [
            jnp.where(y_at == 0, flag(a, 0), jnp.where(y_at == 33, flag(a, 2), flag(a, 1)))
            for a in range(3)
        ]
        bias_one = b1_ref[...]
        bias_two = b2_ref[...]

        def first_conv(z, count):
            rows = [
                ext_ref[z:z + count, t:t + PITCH, :].reshape(count * PITCH, 256).astype(BF)
                for t in range(3)
            ]
            total = jnp.dot(
                jnp.concatenate(rows, axis=1), w1_ref[...], preferred_element_type=F32
            )
            act = jnp.maximum(total + bias_one, 0.0).reshape(count, PITCH, 256)
            for k in range(count):
                zone = 0 if z + k == 0 else 2 if z + k == 33 else 1
                hid_ref[z + k] = act[k] * regions[zone]
            for t in range(3):
                taps_ref[z:z + count, :, t * 256:(t + 1) * 256] = hid_ref[
                    z:z + count, t:t + SIDE, :
                ].astype(BF)

        def second_conv(z):
            rows = [taps_ref[z + a:z + a + 8].reshape(8 * SIDE, 768) for a in range(3)]
            total = jnp.dot(
                jnp.concatenate(rows, axis=1), w2_ref[...], preferred_element_type=F32
            )
            act = jnp.maximum(total + bias_two, 0.0).reshape(4, 2, SIDE, 256)
            act = act[:, 0] + act[:, 1]
            left, right = act[..., :128], act[..., 128:]
            left = left + pltpu.roll(left, 64, 2)
            right = right + pltpu.roll(right, 64, 2)
            pool_ref[z // 2:z // 2 + 4] = jnp.where(low, left, right)

        put_rim(0, 0, 0)
        put_main(0)
        put_main(1)
        first_conv(0, 9)
        put_main(2)
        put_main(3)
        first_conv(9, 8)
        second_conv(0)
        put_main(4)
        put_main(5)
        first_conv(17, 8)
        second_conv(8)
        put_main(6)
        put_main(7)
        put_rim(1, 2, 33)
        first_conv(25, 9)
        second_conv(16)
        second_conv(24)
        pooled = pool_ref[:, pl.ds(0, 16, stride=2), :] + pool_ref[:, pl.ds(1, 16, stride=2), :]
        pooled = (pooled * 0.125).reshape(256, 128)
        turned = jnp.transpose(pooled).astype(BF)
        result = jnp.dot(turned[:64], inter_ref[0], preferred_element_type=F32)
        result = result + jnp.dot(turned[64:], inter_ref[1], preferred_element_type=F32)
        out_ref[0] = result.astype(BF)


def compute_bricks(
    count, cols, slots, flags, volume, zhalo, edge, w1, b1, w2, b2, out_slots, columns, steps
):
    spread = jnp.asarray(spread_matrix(), BF)
    inter = jnp.asarray(interleave_matrices(), BF)

    def at(shift):
        def index(i, n, c, s, f):
            return (0, 0, jnp.clip(c[i] + shift, 0, columns - 1))
        return index

    def whole(shape):
        return pl.BlockSpec(shape, lambda i, n, c, s, f: (0,) * len(shape))

    grid_spec = pltpu.PrefetchScalarGridSpec(
        num_scalar_prefetch=4,
        grid=(steps,),
        in_specs=[pl.BlockSpec((SIDE, 64, 128), at(s)) for s in (0, -1, 1)]
        + [pl.BlockSpec((2, 64, 128), at(s)) for s in (0, -1, 1)]
        + [whole(v.shape) for v in (edge, spread, inter, w1, b1, w2, b2)],
        out_specs=pl.BlockSpec((1, 64, 512), lambda i, n, c, s, f: (s[i], 0, 0)),
        scratch_shapes=[
            pltpu.VMEM((34, 48, 256), F32),
            pltpu.VMEM((34, PITCH, 256), F32),
            pltpu.VMEM((34, SIDE, 768), BF),
            pltpu.VMEM((16, SIDE, 128), F32),
        ],
    )
    return pl.pallas_call(
        functools.partial(brick_kernel, columns=columns),
        out_shape=jax.ShapeDtypeStruct((out_slots, 64, 512), BF),
        grid_spec=grid_spec,
        compiler_params=pltpu.CompilerParams(
            dimension_semantics=("arbitrary",), vmem_limit_bytes=48 * 1024 * 1024
        ),
        cost_estimate=pl.CostEstimate(
            flops=steps * 1_600_000_000, bytes_accessed=steps * 1_600_000, transcendentals=0
        ),
    )(count, cols, slots, flags, volume, volume, volume, zhalo, zhalo, zhalo, edge,
      spread, inter, w1, b1, w2, b2)


def per_device(volume, occupancy, device_order, weight_one, bias_one, weight_two, bias_two):
    columns = occupancy.shape[1]
    slabs = lax.axis_size("gz")
    groups = lax.axis_size("xy")
    capacity = (columns + groups - 1) // groups
    slot_count = columns // 2
    me_z = lax.axis_index("gz")
    me = lax.axis_index("xy")
    rims = 2 * ACROSS

    up_z = [(i, i + 1) for i in range(slabs - 1)]
    down_z = [(j, i) for i, j in up_z]
    up_y = [(i, i + 1) for i in range(groups - 1)]
    down_y = [(j, i) for i, j in up_y]
    below = lax.ppermute(volume[SIDE - 1:], "gz", up_z)
    above = lax.ppermute(volume[:1], "gz", down_z)
    zhalo = jnp.concatenate([below, above], axis=0)
    span = volume.shape[2]
    tail = jnp.concatenate([volume[:, :, span - rims:], zhalo[:, :, span - rims:]], axis=0)
    head = jnp.concatenate([volume[:, :, :rims], zhalo[:, :, :rims]], axis=0)
    layers = tail.shape[0]
    before = lax.ppermute(tail.reshape(layers, -1), "xy", up_y).reshape(layers, 64, rims)
    after = lax.ppermute(head.reshape(layers, -1), "xy", down_y).reshape(layers, 64, rims)
    edge = jnp.concatenate(
        [after, jnp.zeros((layers, 64, 128 - 2 * rims), BF), before], axis=2
    )

    table = lax.all_gather(occupancy, ("gz", "xy"), axis=0, tiled=True)
    table = table.reshape(slabs, groups * columns)
    total = groups * columns
    marks = jnp.pad(table, ((1, 1), (1, 1)))
    near = lax.dynamic_slice(marks, (me_z, me * columns), (3, columns + 2))
    row = lax.dynamic_slice(table, (me_z, 0), (1, total))[0]
    own = occupancy[0]
    order = device_order[0]
    ids = jnp.arange(columns, dtype=jnp.int32)
    labels = jnp.arange(groups, dtype=jnp.int32)
    everyone = jnp.arange(total, dtype=jnp.int32)
    local_rank = jnp.sum(jnp.where(ids[None, :] < ids[:, None], own[None, :], 0), axis=1)
    start = jnp.sum(jnp.where(everyone < me * columns, row, 0))
    label = (start + local_rank) % groups
    target = jnp.sum(jnp.where(label[:, None] == labels[None, :], order[None, :], 0), axis=1)
    count = jnp.sum(own)
    flag_of = jnp.stack([near[a, b:b + columns] for a in range(3) for b in range(3)], axis=1)
    early = min(columns, 2 * groups)

    def part(begin, end):
        amount = jnp.clip(count - begin, 0, end - begin)
        wanted = begin + jnp.minimum(
            jnp.arange(end - begin, dtype=jnp.int32), jnp.maximum(amount - 1, 0)
        )
        hit = (local_rank[None, :] == wanted[:, None]) & (own[None, :] > 0)
        cols = jnp.sum(jnp.where(hit, ids[None, :], 0), axis=1)
        part_capacity = (end - begin + groups - 1) // groups
        slot = target * part_capacity + (local_rank - begin) // groups
        slots = jnp.sum(jnp.where(hit, slot[None, :], 0), axis=1)
        flags = jnp.sum(jnp.where(hit[:, :, None], flag_of[None], 0), axis=1).reshape(-1)
        return amount.reshape(1), cols, slots, flags, part_capacity

    w1 = banded(weight_one.reshape(64, 3, 3, 64).transpose(1, 2, 3, 0)).reshape(768, 256)
    w2 = banded(weight_two.reshape(64, 3, 3, 3, 64).transpose(1, 2, 3, 4, 0)).reshape(2304, 256)
    b1 = jnp.tile(bias_one, ACROSS)[None]
    b2 = jnp.tile(bias_two, ACROSS)[None]

    arrived = []
    for begin, end in ((0, early), (early, columns)):
        if begin < end:
            amount, cols, slots, flags, part_capacity = part(begin, end)
            made = compute_bricks(
                amount, cols, slots, flags, volume, zhalo, edge, w1, b1, w2, b2,
                groups * part_capacity, columns, end - begin,
            )
            sent = lax.all_to_all(made, "xy", split_axis=0, concat_axis=0, tiled=True)
            arrived.append(sent.reshape(groups, part_capacity, 64, 512))
    arrived = jnp.concatenate(arrived, axis=1).reshape(groups * capacity, 64, 512)

    my_label = jnp.sum(jnp.where(order == me, labels, 0))
    need = jnp.arange(slot_count, dtype=jnp.int32) * groups + my_label
    counts = row.reshape(groups, columns).sum(axis=1)
    starts = jnp.sum(jnp.where(labels[None, :] < labels[:, None], counts[None, :], 0), axis=1)
    owner = jnp.sum(((starts + counts)[None, :] <= need[:, None]).astype(jnp.int32), axis=1)
    owner_start = jnp.sum(jnp.where(labels[None, :] == owner[:, None], starts[None, :], 0), axis=1)
    arrival = owner * capacity + (need - owner_start) // groups
    return jnp.take(arrived, arrival, axis=0)


def solution(mesh):
    in_specs = (P("gz", None, "xy"), P("gz", "xy"), P("gz", None), P(), P(), P(), P())
    out_specs = P(("gz", "xy"), None, None)
    return jax.shard_map(
        per_device, mesh=mesh, in_specs=in_specs, out_specs=out_specs, check_vma=False
    )
```

```python
import functools

import numpy as np
import jax
import jax.numpy as jnp
from jax import lax
from jax.experimental import pallas as pl
from jax.experimental.pallas import tpu as pltpu
from jax.sharding import PartitionSpec as P

BF = jnp.bfloat16
F32 = jnp.float32
SIDE = 32
ACROSS = 4
PITCH = 40


def spread_matrix():
    table = np.zeros((ACROSS * PITCH, 256), np.float32)
    for x in range(ACROSS):
        for y in range(SIDE):
            table[x * PITCH + y + 2, y * ACROSS + x] = 1
        for y in range(2):
            table[x * PITCH + 34 + y, 128 + y * ACROSS + x] = 1
            table[x * PITCH + y, 128 + (30 + y) * ACROSS + x] = 1
    return table


def interleave_matrices():
    table = np.zeros((2, 256, 512), np.float32)
    for x in range(2):
        table[x, np.arange(256), np.arange(256) * 2 + x] = 1
    return table


def banded(taps):
    zero = jnp.zeros_like(taps[..., 0, :, :])
    rows = []
    for xi in range(ACROSS):
        blocks = []
        for xo in range(ACROSS):
            tap = xi - xo + 1
            blocks.append(taps[..., tap, :, :] if 0 <= tap < 3 else zero)
        rows.append(jnp.concatenate(blocks, axis=-1))
    return jnp.concatenate(rows, axis=-2)


def brick_kernel(
    n_ref, cols_ref, slots_ref, flags_ref,
    main_ref, prev_ref, next_ref, zmain_ref, zprev_ref, znext_ref, edge_ref,
    spread_ref, inter_ref, w1_ref, b1_ref, w2_ref, b2_ref,
    out_ref,
    ext_ref, hid_ref, taps_ref, pool_ref,
    *, columns,
):
    step = pl.program_id(0)

    @pl.when(step < n_ref[0])
    def _():
        col = cols_ref[step]
        first = col == 0
        last = col == columns - 1

        def flag(a, b):
            return flags_ref[step * 9 + 3 * a + b].astype(F32)

        lane = lax.broadcasted_iota(jnp.int32, (1, 1, 128), 2)
        low = lane < 64
        from_edge = jnp.where(low, last.astype(jnp.int32), first.astype(jnp.int32)) > 0

        def keep(value, mark):
            return jnp.where(mark > 0, value, jnp.zeros((), BF))

        def rim(before, after, edge, a):
            value = jnp.where(from_edge, edge, jnp.where(low, after, before))
            return keep(value, jnp.where(low, flag(a, 2), flag(a, 0)))

        spread = spread_ref[...]

        def put(own, side, first_layer):
            count = own.shape[0]
            both = jnp.concatenate(
                [own.reshape(count * 64, 128), side.reshape(count * 64, 128)], axis=1
            )
            turned = lax.dot_general(
                spread, both, (((1,), (1,)), ((), ())), preferred_element_type=F32
            )
            for k in range(count):
                for half in range(2):
                    pieces = [
                        turned[x * PITCH:(x + 1) * PITCH, k * 64:(k + 1) * 64]
                        for x in (2 * half, 2 * half + 1)
                    ]
                    ext_ref[first_layer + k, 0:PITCH, half * 128:(half + 1) * 128] = (
                        jnp.concatenate(pieces, axis=1)
                    )

        def put_main(k):
            at = slice(4 * k, 4 * k + 4)
            put(main_ref[at], rim(prev_ref[at], next_ref[at], edge_ref[at], 1), 4 * k + 1)

        def put_rim(layer, a, spot):
            at = slice(layer, layer + 1)
            side = rim(zprev_ref[at], znext_ref[at], edge_ref[32 + layer:33 + layer], a)
            put(keep(zmain_ref[at], flag(a, 1)), side, spot)

        y_at = lax.broadcasted_iota(jnp.int32, (PITCH, 256), 0)
        regions = [
            jnp.where(y_at == 0, flag(a, 0), jnp.where(y_at == 33, flag(a, 2), flag(a, 1)))
            for a in range(3)
        ]
        bias_one = b1_ref[...]
        bias_two = b2_ref[...]

        def first_conv(z, count):
            rows = [
                ext_ref[z:z + count, t:t + PITCH, :].reshape(count * PITCH, 256).astype(BF)
                for t in range(3)
            ]
            total = jnp.dot(
                jnp.concatenate(rows, axis=1), w1_ref[...], preferred_element_type=F32
            )
            act = jnp.maximum(total + bias_one, 0.0).reshape(count, PITCH, 256)
            for k in range(count):
                zone = 0 if z + k == 0 else 2 if z + k == 33 else 1
                hid_ref[z + k] = act[k] * regions[zone]
            for t in range(3):
                taps_ref[z:z + count, :, t * 256:(t + 1) * 256] = hid_ref[
                    z:z + count, t:t + SIDE, :
                ].astype(BF)

        def second_conv(z):
            rows = [taps_ref[z + a:z + a + 8].reshape(8 * SIDE, 768) for a in range(3)]
            total = jnp.dot(
                jnp.concatenate(rows, axis=1), w2_ref[...], preferred_element_type=F32
            )
            act = jnp.maximum(total + bias_two, 0.0).reshape(4, 2, SIDE, 256)
            act = act[:, 0] + act[:, 1]
            left, right = act[..., :128], act[..., 128:]
            left = left + pltpu.roll(left, 64, 2)
            right = right + pltpu.roll(right, 64, 2)
            pool_ref[z // 2:z // 2 + 4] = jnp.where(low, left, right)

        put_rim(0, 0, 0)
        put_main(0)
        put_main(1)
        first_conv(0, 9)
        put_main(2)
        put_main(3)
        first_conv(9, 8)
        second_conv(0)
        put_main(4)
        put_main(5)
        first_conv(17, 8)
        second_conv(8)
        put_main(6)
        put_main(7)
        put_rim(1, 2, 33)
        first_conv(25, 9)
        second_conv(16)
        second_conv(24)
        pooled = pool_ref[:, pl.ds(0, 16, stride=2), :] + pool_ref[:, pl.ds(1, 16, stride=2), :]
        pooled = (pooled * 0.125).reshape(256, 128)
        turned = jnp.transpose(pooled).astype(BF)
        result = jnp.dot(turned[:64], inter_ref[0], preferred_element_type=F32)
        result = result + jnp.dot(turned[64:], inter_ref[1], preferred_element_type=F32)
        out_ref[0] = result.astype(BF)


def compute_bricks(
    count, cols, slots, flags, volume, zhalo, edge, w1, b1, w2, b2, out_slots, columns, steps
):
    spread = jnp.asarray(spread_matrix(), BF)
    inter = jnp.asarray(interleave_matrices(), BF)

    def at(shift):
        def index(i, n, c, s, f):
            return (0, 0, jnp.clip(c[i] + shift, 0, columns - 1))
        return index

    def whole(shape):
        return pl.BlockSpec(shape, lambda i, n, c, s, f: (0,) * len(shape))

    grid_spec = pltpu.PrefetchScalarGridSpec(
        num_scalar_prefetch=4,
        grid=(steps,),
        in_specs=[pl.BlockSpec((SIDE, 64, 128), at(s)) for s in (0, -1, 1)]
        + [pl.BlockSpec((2, 64, 128), at(s)) for s in (0, -1, 1)]
        + [whole(v.shape) for v in (edge, spread, inter, w1, b1, w2, b2)],
        out_specs=pl.BlockSpec((1, 64, 512), lambda i, n, c, s, f: (s[i], 0, 0)),
        scratch_shapes=[
            pltpu.VMEM((34, 48, 256), F32),
            pltpu.VMEM((34, PITCH, 256), F32),
            pltpu.VMEM((34, SIDE, 768), BF),
            pltpu.VMEM((16, SIDE, 128), F32),
        ],
    )
    return pl.pallas_call(
        functools.partial(brick_kernel, columns=columns),
        out_shape=jax.ShapeDtypeStruct((out_slots, 64, 512), BF),
        grid_spec=grid_spec,
        compiler_params=pltpu.CompilerParams(
            dimension_semantics=("arbitrary",), vmem_limit_bytes=48 * 1024 * 1024
        ),
        cost_estimate=pl.CostEstimate(
            flops=steps * 1_600_000_000, bytes_accessed=steps * 1_600_000, transcendentals=0
        ),
    )(count, cols, slots, flags, volume, volume, volume, zhalo, zhalo, zhalo, edge,
      spread, inter, w1, b1, w2, b2)


MESH = pl.DeviceIdType.MESH


def exchange_kernel(
    volume_ref, occ_ref, zhalo_ref, edge_ref, table_ref, near_ref,
    head_ref, tail_ref, packed_ref, landed_ref, corner_ref, occ_out_ref,
    local_sem, occ_send, occ_recv, near_send, near_recv, rim_send, rim_recv,
    *, slabs, groups, columns,
):
    gz = lax.axis_index("gz")
    xy = lax.axis_index("xy")
    span = volume_ref.shape[2]

    def exists(dz, dy):
        return (gz + dz >= 0) & (gz + dz < slabs) & (xy + dy >= 0) & (xy + dy < groups)

    around = [(dz, dy) for dz in (-1, 0, 1) for dy in (-1, 0, 1) if (dz, dy) != (0, 0)]
    local = [
        pltpu.make_async_copy(volume_ref.at[:, :, pl.ds(0, 128)], head_ref, local_sem.at[0]),
        pltpu.make_async_copy(
            volume_ref.at[:, :, pl.ds(span - 128, 128)], tail_ref, local_sem.at[1]
        ),
    ]
    for copy in local:
        copy.start()

    occ_out_ref[...] = jnp.zeros((8, 128), jnp.int32)
    occ_out_ref[0:1, 0:columns] = occ_ref[...]
    near_ref[...] = jnp.zeros((3, 3, 8, 128), jnp.int32)
    near_ref[1, 1] = occ_out_ref[...]
    landed_ref[...] = jnp.zeros_like(landed_ref)
    corner_ref[...] = jnp.zeros_like(corner_ref)
    table_ref[xy] = occ_out_ref[...]

    barrier = pltpu.get_barrier_semaphore()
    partners = groups - 1
    for step in range(1, groups):
        pl.semaphore_signal(
            barrier, inc=1, device_id=(gz, lax.rem(xy + step, groups)), device_id_type=MESH
        )
    for dz, dy in around:
        if dz != 0:
            partners = partners + exists(dz, dy).astype(jnp.int32)

            @pl.when(exists(dz, dy))
            def _(dz=dz, dy=dy):
                pl.semaphore_signal(
                    barrier, inc=1, device_id=(gz + dz, xy + dy), device_id_type=MESH
                )

    pl.semaphore_wait(barrier, partners)

    marks = []
    for step in range(1, groups):
        marks.append(pltpu.make_async_remote_copy(
            src_ref=occ_out_ref, dst_ref=table_ref.at[xy],
            send_sem=occ_send.at[step], recv_sem=occ_recv.at[step],
            device_id=(gz, lax.rem(xy + step, groups)), device_id_type=MESH,
        ))
        marks[-1].start()

    guarded = []

    def send(dz, dy, src, dst, send_sem, recv_sem):
        copy = pltpu.make_async_remote_copy(
            src_ref=src, dst_ref=dst, send_sem=send_sem, recv_sem=recv_sem,
            device_id=(gz + dz, xy + dy), device_id_type=MESH,
        )
        pl.when(exists(dz, dy))(copy.start)
        guarded.append((dz, dy, copy))

    send(1, 0, volume_ref.at[SIDE - 1], zhalo_ref.at[0], rim_send.at[0], rim_recv.at[0])
    send(-1, 0, volume_ref.at[0], zhalo_ref.at[1], rim_send.at[1], rim_recv.at[1])
    for k, (dz, dy) in enumerate(around):
        send(
            dz, dy, occ_out_ref, near_ref.at[1 - dz, 1 - dy], near_send.at[k], near_recv.at[k]
        )
    for copy in local:
        copy.wait()
    corners = (
        (1, 1, tail_ref, SIDE - 1), (1, -1, head_ref, SIDE - 1),
        (-1, 1, tail_ref, 0), (-1, -1, head_ref, 0),
    )
    for k, (dz, dy, source, layer) in enumerate(corners):
        send(dz, dy, source.at[layer], corner_ref.at[k], rim_send.at[2 + k], rim_recv.at[2 + k])

    lane = lax.broadcasted_iota(jnp.int32, (1, 128), 1)
    for which, source, origin in ((0, tail_ref, 120), (1, head_ref, 0)):
        for group in range(2):
            packed = jnp.zeros((64, 128), F32)
            for k in range(16):
                value = source[group * 16 + k].astype(F32)
                shift = (8 * k - origin) % 128
                value = pltpu.roll(value, shift, 1) if shift else value
                packed = jnp.where((lane >= 8 * k) & (lane < 8 * k + 8), value, packed)
            packed_ref[which, group] = packed.astype(BF)
    for which, dy in ((0, 1), (1, -1)):
        send(
            0, dy, packed_ref.at[which], landed_ref.at[which],
            rim_send.at[6 + which], rim_recv.at[6 + which],
        )

    for dz, dy, copy in guarded:
        pl.when(exists(-dz, -dy))(copy.wait_recv)
    for copy in marks:
        copy.wait_recv()

    zero = jnp.zeros((64, 128), F32)
    for group in range(2):
        before = landed_ref[0, group].astype(F32)
        after = landed_ref[1, group].astype(F32)
        for k in range(16):
            up = (120 - 8 * k) % 128
            down = (-8 * k) % 128
            left = pltpu.roll(before, up, 1) if up else before
            right = pltpu.roll(after, down, 1) if down else after
            value = jnp.where(lane < 8, right, jnp.where(lane >= 120, left, zero))
            edge_ref[group * 16 + k] = value.astype(BF)
    for layer in range(2):
        left = corner_ref[2 * layer].astype(F32)
        right = corner_ref[2 * layer + 1].astype(F32)
        value = jnp.where(lane < 8, right, jnp.where(lane >= 120, left, zero))
        edge_ref[SIDE + layer] = value.astype(BF)

    for dz, dy, copy in guarded:
        pl.when(exists(dz, dy))(copy.wait_send)
    for copy in marks:
        copy.wait_send()


def exchange(volume, occupancy, slabs, groups, columns):
    vmem = pl.BlockSpec(memory_space=pltpu.VMEM)
    anywhere = pl.BlockSpec(memory_space=pl.ANY)
    dma = pltpu.SemaphoreType.DMA
    return pl.pallas_call(
        functools.partial(exchange_kernel, slabs=slabs, groups=groups, columns=columns),
        out_shape=(
            jax.ShapeDtypeStruct((2,) + volume.shape[1:], BF),
            jax.ShapeDtypeStruct((SIDE + 2, 64, 128), BF),
            jax.ShapeDtypeStruct((groups, 8, 128), jnp.int32),
            jax.ShapeDtypeStruct((3, 3, 8, 128), jnp.int32),
        ),
        in_specs=[anywhere, vmem],
        out_specs=(anywhere, vmem, vmem, vmem),
        scratch_shapes=[
            pltpu.VMEM((SIDE, 64, 128), BF),
            pltpu.VMEM((SIDE, 64, 128), BF),
            pltpu.VMEM((2, 2, 64, 128), BF),
            pltpu.VMEM((2, 2, 64, 128), BF),
            pltpu.VMEM((4, 64, 128), BF),
            pltpu.VMEM((8, 128), jnp.int32),
            dma((2,)), dma((groups,)), dma((groups,)), dma((8,)), dma((8,)), dma((8,)), dma((8,)),
        ],
        compiler_params=pltpu.CompilerParams(
            collective_id=0, has_side_effects=True, vmem_limit_bytes=16 * 1024 * 1024
        ),
        cost_estimate=pl.CostEstimate(flops=0, bytes_accessed=2_000_000, transcendentals=0),
    )(volume, occupancy)


def per_device(volume, occupancy, device_order, weight_one, bias_one, weight_two, bias_two):
    columns = occupancy.shape[1]
    slabs = lax.axis_size("gz")
    groups = lax.axis_size("xy")
    capacity = (columns + groups - 1) // groups
    slot_count = columns // 2
    me = lax.axis_index("xy")
    zhalo, edge, table, near = exchange(volume, occupancy, slabs, groups, columns)
    total = groups * columns
    row = table[:, 0, :columns].reshape(total)
    near = near[:, :, 0, :columns].reshape(3, 3 * columns)[:, columns - 1:2 * columns + 1]
    own = occupancy[0]
    order = device_order[0]
    ids = jnp.arange(columns, dtype=jnp.int32)
    labels = jnp.arange(groups, dtype=jnp.int32)
    everyone = jnp.arange(total, dtype=jnp.int32)
    local_rank = jnp.sum(jnp.where(ids[None, :] < ids[:, None], own[None, :], 0), axis=1)
    start = jnp.sum(jnp.where(everyone < me * columns, row, 0))
    label = (start + local_rank) % groups
    target = jnp.sum(jnp.where(label[:, None] == labels[None, :], order[None, :], 0), axis=1)
    count = jnp.sum(own)
    flag_of = jnp.stack([near[a, b:b + columns] for a in range(3) for b in range(3)], axis=1)
    early = min(columns, 2 * groups)

    def part(begin, end):
        amount = jnp.clip(count - begin, 0, end - begin)
        wanted = begin + jnp.minimum(
            jnp.arange(end - begin, dtype=jnp.int32), jnp.maximum(amount - 1, 0)
        )
        hit = (local_rank[None, :] == wanted[:, None]) & (own[None, :] > 0)
        cols = jnp.sum(jnp.where(hit, ids[None, :], 0), axis=1)
        part_capacity = (end - begin + groups - 1) // groups
        slot = target * part_capacity + (local_rank - begin) // groups
        slots = jnp.sum(jnp.where(hit, slot[None, :], 0), axis=1)
        flags = jnp.sum(jnp.where(hit[:, :, None], flag_of[None], 0), axis=1).reshape(-1)
        return amount.reshape(1), cols, slots, flags, part_capacity

    w1 = banded(weight_one.reshape(64, 3, 3, 64).transpose(1, 2, 3, 0)).reshape(768, 256)
    w2 = banded(weight_two.reshape(64, 3, 3, 3, 64).transpose(1, 2, 3, 4, 0)).reshape(2304, 256)
    b1 = jnp.tile(bias_one, ACROSS)[None]
    b2 = jnp.tile(bias_two, ACROSS)[None]

    arrived = []
    for begin, end in ((0, early), (early, columns)):
        if begin < end:
            amount, cols, slots, flags, part_capacity = part(begin, end)
            made = compute_bricks(
                amount, cols, slots, flags, volume, zhalo, edge, w1, b1, w2, b2,
                groups * part_capacity, columns, end - begin,
            )
            sent = lax.all_to_all(made, "xy", split_axis=0, concat_axis=0, tiled=True)
            arrived.append(sent.reshape(groups, part_capacity, 64, 512))
    arrived = jnp.concatenate(arrived, axis=1).reshape(groups * capacity, 64, 512)

    my_label = jnp.sum(jnp.where(order == me, labels, 0))
    need = jnp.arange(slot_count, dtype=jnp.int32) * groups + my_label
    counts = row.reshape(groups, columns).sum(axis=1)
    starts = jnp.sum(jnp.where(labels[None, :] < labels[:, None], counts[None, :], 0), axis=1)
    owner = jnp.sum(((starts + counts)[None, :] <= need[:, None]).astype(jnp.int32), axis=1)
    owner_start = jnp.sum(jnp.where(labels[None, :] == owner[:, None], starts[None, :], 0), axis=1)
    arrival = owner * capacity + (need - owner_start) // groups
    return jnp.take(arrived, arrival, axis=0)


def solution(mesh):
    in_specs = (P("gz", None, "xy"), P("gz", "xy"), P("gz", None), P(), P(), P(), P())
    out_specs = P(("gz", "xy"), None, None)
    return jax.shard_map(
        per_device, mesh=mesh, in_specs=in_specs, out_specs=out_specs, check_vma=False
    )
```

```python
import functools

import numpy as np
import jax
import jax.numpy as jnp
from jax import lax
from jax.experimental import pallas as pl
from jax.experimental.pallas import tpu as pltpu
from jax.sharding import PartitionSpec as P

BF = jnp.bfloat16
F32 = jnp.float32
SIDE = 32
ACROSS = 4
PITCH = 40


def spread_matrix():
    table = np.zeros((ACROSS * PITCH, 256), np.float32)
    for x in range(ACROSS):
        for y in range(SIDE):
            table[x * PITCH + y + 2, y * ACROSS + x] = 1
        for y in range(2):
            table[x * PITCH + 34 + y, 128 + y * ACROSS + x] = 1
            table[x * PITCH + y, 128 + (30 + y) * ACROSS + x] = 1
    return table


def interleave_matrices():
    table = np.zeros((2, 256, 512), np.float32)
    for x in range(2):
        table[x, np.arange(256), np.arange(256) * 2 + x] = 1
    return table


def plan_kernel(
    table_ref, near_ref, order_ref, w1_ref, b1_ref, w2_ref, b2_ref,
    count_ref, cols_ref, slots_ref, flags_ref, owner_ref, part_ref,
    band1_ref, wide1_ref, band2_ref, wide2_ref, start_ref,
    *, groups, columns,
):
    xy = lax.axis_index("xy")

    def tally(g, before):
        start_ref[g] = before
        return lax.fori_loop(0, columns, lambda j, t: t + table_ref[g, 0, j], before)

    start_ref[groups] = lax.fori_loop(0, groups, tally, jnp.int32(0))
    first = start_ref[xy]

    def place(j, rank):
        label = lax.rem(first + rank, groups)
        cols_ref[rank] = j
        slots_ref[rank] = order_ref[0, label]
        for b in range(3):
            at = j + b - 1
            block = jnp.where(at < 0, 0, jnp.where(at >= columns, 2, 1))
            spot = jnp.where(at < 0, columns - 1, jnp.where(at >= columns, 0, at))
            for a in range(3):
                flags_ref[rank * 9 + 3 * a + b] = near_ref[a, block, 0, spot]
        return rank + table_ref[xy, 0, j]

    slots_ref[0] = 0
    count = lax.fori_loop(0, columns, place, jnp.int32(0))
    count_ref[0] = count
    last = jnp.maximum(count - 1, 0)

    def repeat(i, carry):
        cols_ref[i] = cols_ref[last]
        slots_ref[i] = slots_ref[last]
        return carry

    lax.fori_loop(count, columns, repeat, 0)

    mine = lax.fori_loop(
        0, groups, lambda g, t: jnp.where(order_ref[0, g] == xy, g, t), jnp.int32(0)
    )

    def arrive(k, carry):
        need = k * groups + mine
        owner = lax.fori_loop(
            1, groups, lambda g, t: t + (start_ref[g] <= need).astype(jnp.int32), jnp.int32(0)
        )
        owner_ref[k] = owner
        part_ref[k] = (need - start_ref[owner]) // groups
        return carry

    lax.fori_loop(0, columns // 2, arrive, 0)

    zero = jnp.zeros((64, 64), BF)
    for source, band in ((w1_ref, band1_ref), (w2_ref, band2_ref)):
        for row in range(source.shape[0] // 192):
            taps = [source[(3 * row + t) * 64:(3 * row + t + 1) * 64, :] for t in range(3)]
            for xi in range(ACROSS):
                blocks = [
                    taps[xi - xo + 1] if 0 <= xi - xo + 1 < 3 else zero for xo in range(ACROSS)
                ]
                at = (ACROSS * row + xi) * 64
                band[at:at + 64, :] = jnp.concatenate(blocks, axis=1)
    wide1_ref[...] = jnp.concatenate([b1_ref[...]] * ACROSS, axis=1)
    wide2_ref[...] = jnp.concatenate([b2_ref[...]] * ACROSS, axis=1)


def plan(table, near, order, weight_one, bias_one, weight_two, bias_two, groups, columns):
    vmem = pl.BlockSpec(memory_space=pltpu.VMEM)
    smem = pl.BlockSpec(memory_space=pltpu.SMEM)

    def ints(length):
        return jax.ShapeDtypeStruct((length,), jnp.int32)

    return pl.pallas_call(
        functools.partial(plan_kernel, groups=groups, columns=columns),
        out_shape=(
            ints(1), ints(columns + 1), ints(columns + 1), ints(9 * columns + 9),
            ints(columns // 2), ints(columns // 2),
            jax.ShapeDtypeStruct((768, 256), BF), jax.ShapeDtypeStruct((1, 256), F32),
            jax.ShapeDtypeStruct((2304, 256), BF), jax.ShapeDtypeStruct((1, 256), F32),
        ),
        in_specs=[smem] * 3 + [vmem] * 4,
        out_specs=(smem,) * 6 + (vmem,) * 4,
        scratch_shapes=[pltpu.SMEM((groups + 1,), jnp.int32)],
        cost_estimate=pl.CostEstimate(flops=0, bytes_accessed=4_000_000, transcendentals=0),
    )(table, near, order, weight_one.T, bias_one[None], weight_two.T, bias_two[None])


def collect_kernel(owner_ref, part_ref, *refs):
    sources, out_ref, sems = refs[:-2], refs[-2], refs[-1]
    for k in range(out_ref.shape[0]):
        for which, source in enumerate(sources):
            @pl.when(part_ref[k] == which)
            def _(k=k, source=source):
                pltpu.make_async_copy(
                    source.at[owner_ref[k]], out_ref.at[k], sems.at[k]
                ).start()
    for k in range(out_ref.shape[0]):
        pltpu.make_async_copy(sources[0].at[0], out_ref.at[k], sems.at[k]).wait()


def collect(owner, part, arrived, slot_count):
    smem = pl.BlockSpec(memory_space=pltpu.SMEM)
    anywhere = pl.BlockSpec(memory_space=pl.ANY)
    return pl.pallas_call(
        collect_kernel,
        out_shape=jax.ShapeDtypeStruct((slot_count, 64, 512), BF),
        in_specs=[smem, smem] + [anywhere] * len(arrived),
        out_specs=anywhere,
        scratch_shapes=[pltpu.SemaphoreType.DMA((slot_count,))],
    )(owner, part, *arrived)


def brick_kernel(
    n_ref, cols_ref, slots_ref, flags_ref,
    main_ref, prev_ref, next_ref, zmain_ref, zprev_ref, znext_ref, edge_ref,
    spread_ref, inter_ref, w1_ref, b1_ref, w2_ref, b2_ref, *refs,
    columns, begin,
):
    out_ref, ext_ref, hid_ref, taps_ref, pool_ref = refs[-5:]
    step = pl.program_id(0) + begin

    @pl.when(step < n_ref[0])
    def _():
        col = cols_ref[step]
        first = col == 0
        last = col == columns - 1

        def flag(a, b):
            return flags_ref[step * 9 + 3 * a + b].astype(F32)

        lane = lax.broadcasted_iota(jnp.int32, (1, 1, 128), 2)
        low = lane < 64
        from_edge = jnp.where(low, last.astype(jnp.int32), first.astype(jnp.int32)) > 0

        def keep(value, mark):
            return jnp.where(mark > 0, value, jnp.zeros((), BF))

        def rim(before, after, edge, a):
            value = jnp.where(from_edge, edge, jnp.where(low, after, before))
            return keep(value, jnp.where(low, flag(a, 2), flag(a, 0)))

        spread = spread_ref[...]

        def put(own, side, first_layer):
            count = own.shape[0]
            both = jnp.concatenate(
                [own.reshape(count * 64, 128), side.reshape(count * 64, 128)], axis=1
            )
            turned = lax.dot_general(
                spread, both, (((1,), (1,)), ((), ())), preferred_element_type=F32
            )
            for k in range(count):
                for half in range(2):
                    pieces = [
                        turned[x * PITCH:(x + 1) * PITCH, k * 64:(k + 1) * 64]
                        for x in (2 * half, 2 * half + 1)
                    ]
                    ext_ref[first_layer + k, 0:PITCH, half * 128:(half + 1) * 128] = (
                        jnp.concatenate(pieces, axis=1)
                    )

        def put_main(k):
            at = slice(4 * k, 4 * k + 4)
            put(main_ref[at], rim(prev_ref[at], next_ref[at], edge_ref[at], 1), 4 * k + 1)

        def put_rim(layer, a, spot):
            at = slice(layer, layer + 1)
            side = rim(zprev_ref[at], znext_ref[at], edge_ref[32 + layer:33 + layer], a)
            put(keep(zmain_ref[at], flag(a, 1)), side, spot)

        y_at = lax.broadcasted_iota(jnp.int32, (PITCH, 256), 0)
        regions = [
            jnp.where(y_at == 0, flag(a, 0), jnp.where(y_at == 33, flag(a, 2), flag(a, 1)))
            for a in range(3)
        ]
        bias_one = b1_ref[...]
        bias_two = b2_ref[...]

        def first_conv(z, count):
            rows = [
                ext_ref[z:z + count, t:t + PITCH, :].reshape(count * PITCH, 256).astype(BF)
                for t in range(3)
            ]
            total = jnp.dot(
                jnp.concatenate(rows, axis=1), w1_ref[...], preferred_element_type=F32
            )
            act = jnp.maximum(total + bias_one, 0.0).reshape(count, PITCH, 256)
            for k in range(count):
                zone = 0 if z + k == 0 else 2 if z + k == 33 else 1
                hid_ref[z + k] = act[k] * regions[zone]
            for t in range(3):
                taps_ref[z:z + count, :, t * 256:(t + 1) * 256] = hid_ref[
                    z:z + count, t:t + SIDE, :
                ].astype(BF)

        def second_conv(z):
            rows = [taps_ref[z + a:z + a + 8].reshape(8 * SIDE, 768) for a in range(3)]
            total = jnp.dot(
                jnp.concatenate(rows, axis=1), w2_ref[...], preferred_element_type=F32
            )
            act = jnp.maximum(total + bias_two, 0.0).reshape(4, 2, SIDE, 256)
            act = act[:, 0] + act[:, 1]
            left, right = act[..., :128], act[..., 128:]
            left = left + pltpu.roll(left, 64, 2)
            right = right + pltpu.roll(right, 64, 2)
            pool_ref[z // 2:z // 2 + 4] = jnp.where(low, left, right)

        put_rim(0, 0, 0)
        put_main(0)
        put_main(1)
        first_conv(0, 9)
        put_main(2)
        put_main(3)
        first_conv(9, 8)
        second_conv(0)
        put_main(4)
        put_main(5)
        first_conv(17, 8)
        second_conv(8)
        put_main(6)
        put_main(7)
        put_rim(1, 2, 33)
        first_conv(25, 9)
        second_conv(16)
        second_conv(24)
        pooled = pool_ref[:, pl.ds(0, 16, stride=2), :] + pool_ref[:, pl.ds(1, 16, stride=2), :]
        pooled = (pooled * 0.125).reshape(256, 128)
        turned = jnp.transpose(pooled).astype(BF)
        result = jnp.dot(turned[:64], inter_ref[0], preferred_element_type=F32)
        result = result + jnp.dot(turned[64:], inter_ref[1], preferred_element_type=F32)
        out_ref[0] = result.astype(BF)


def compute_bricks(
    count, cols, slots, flags, volume, zhalo, edge, w1, b1, w2, b2, earlier,
    groups, columns, begin, steps,
):
    spread = jnp.asarray(spread_matrix(), BF)
    inter = jnp.asarray(interleave_matrices(), BF)

    def at(shift):
        def index(i, n, c, s, f):
            return (0, 0, jnp.clip(c[i + begin] + shift, 0, columns - 1))
        return index

    def whole(shape):
        return pl.BlockSpec(shape, lambda i, n, c, s, f: (0,) * len(shape))

    grid_spec = pltpu.PrefetchScalarGridSpec(
        num_scalar_prefetch=4,
        grid=(steps,),
        in_specs=[pl.BlockSpec((SIDE, 64, 128), at(s)) for s in (0, -1, 1)]
        + [pl.BlockSpec((2, 64, 128), at(s)) for s in (0, -1, 1)]
        + [whole(v.shape) for v in (edge, spread, inter, w1, b1, w2, b2)]
        + [pl.BlockSpec(memory_space=pl.ANY)] * len(earlier),
        out_specs=pl.BlockSpec((1, 64, 512), lambda i, n, c, s, f: (s[i + begin], 0, 0)),
        scratch_shapes=[
            pltpu.VMEM((34, 48, 256), F32),
            pltpu.VMEM((34, PITCH, 256), F32),
            pltpu.VMEM((34, SIDE, 768), BF),
            pltpu.VMEM((16, SIDE, 128), F32),
        ],
    )
    return pl.pallas_call(
        functools.partial(brick_kernel, columns=columns, begin=begin),
        out_shape=jax.ShapeDtypeStruct((groups, 64, 512), BF),
        grid_spec=grid_spec,
        compiler_params=pltpu.CompilerParams(
            dimension_semantics=("arbitrary",), vmem_limit_bytes=48 * 1024 * 1024
        ),
        cost_estimate=pl.CostEstimate(
            flops=steps * 1_600_000_000, bytes_accessed=steps * 1_600_000, transcendentals=0
        ),
    )(count, cols, slots, flags, volume, volume, volume, zhalo, zhalo, zhalo, edge,
      spread, inter, w1, b1, w2, b2, *earlier)


MESH = pl.DeviceIdType.MESH


def exchange_kernel(
    volume_ref, occ_ref, zhalo_ref, edge_ref, table_ref, near_ref,
    head_ref, tail_ref, packed_ref, landed_ref, corner_ref, occ_out_ref,
    local_sem, occ_send, occ_recv, near_send, near_recv, rim_send, rim_recv,
    *, slabs, groups, columns,
):
    gz = lax.axis_index("gz")
    xy = lax.axis_index("xy")
    span = volume_ref.shape[2]

    def exists(dz, dy):
        return (gz + dz >= 0) & (gz + dz < slabs) & (xy + dy >= 0) & (xy + dy < groups)

    around = [(dz, dy) for dz in (-1, 0, 1) for dy in (-1, 0, 1) if (dz, dy) != (0, 0)]
    local = [
        pltpu.make_async_copy(volume_ref.at[:, :, pl.ds(0, 128)], head_ref, local_sem.at[0]),
        pltpu.make_async_copy(
            volume_ref.at[:, :, pl.ds(span - 128, 128)], tail_ref, local_sem.at[1]
        ),
    ]
    for copy in local:
        copy.start()

    occ_out_ref[...] = jnp.zeros((8, 128), jnp.int32)
    occ_out_ref[0:1, 0:columns] = occ_ref[...]
    near_ref[...] = jnp.zeros((3, 3, 8, 128), jnp.int32)
    near_ref[1, 1] = occ_out_ref[...]
    landed_ref[...] = jnp.zeros_like(landed_ref)
    corner_ref[...] = jnp.zeros_like(corner_ref)
    table_ref[xy] = occ_out_ref[...]

    barrier = pltpu.get_barrier_semaphore()
    partners = groups - 1
    for step in range(1, groups):
        pl.semaphore_signal(
            barrier, inc=1, device_id=(gz, lax.rem(xy + step, groups)), device_id_type=MESH
        )
    for dz, dy in around:
        if dz != 0:
            partners = partners + exists(dz, dy).astype(jnp.int32)

            @pl.when(exists(dz, dy))
            def _(dz=dz, dy=dy):
                pl.semaphore_signal(
                    barrier, inc=1, device_id=(gz + dz, xy + dy), device_id_type=MESH
                )

    pl.semaphore_wait(barrier, partners)

    marks = []
    for step in range(1, groups):
        marks.append(pltpu.make_async_remote_copy(
            src_ref=occ_out_ref, dst_ref=table_ref.at[xy],
            send_sem=occ_send.at[step], recv_sem=occ_recv.at[step],
            device_id=(gz, lax.rem(xy + step, groups)), device_id_type=MESH,
        ))
        marks[-1].start()

    guarded = []

    def send(dz, dy, src, dst, send_sem, recv_sem):
        copy = pltpu.make_async_remote_copy(
            src_ref=src, dst_ref=dst, send_sem=send_sem, recv_sem=recv_sem,
            device_id=(gz + dz, xy + dy), device_id_type=MESH,
        )
        pl.when(exists(dz, dy))(copy.start)
        guarded.append((dz, dy, copy))

    send(1, 0, volume_ref.at[SIDE - 1], zhalo_ref.at[0], rim_send.at[0], rim_recv.at[0])
    send(-1, 0, volume_ref.at[0], zhalo_ref.at[1], rim_send.at[1], rim_recv.at[1])
    for k, (dz, dy) in enumerate(around):
        send(
            dz, dy, occ_out_ref, near_ref.at[1 - dz, 1 - dy], near_send.at[k], near_recv.at[k]
        )
    for copy in local:
        copy.wait()
    corners = (
        (1, 1, tail_ref, SIDE - 1), (1, -1, head_ref, SIDE - 1),
        (-1, 1, tail_ref, 0), (-1, -1, head_ref, 0),
    )
    for k, (dz, dy, source, layer) in enumerate(corners):
        send(dz, dy, source.at[layer], corner_ref.at[k], rim_send.at[2 + k], rim_recv.at[2 + k])

    lane = lax.broadcasted_iota(jnp.int32, (1, 128), 1)
    for which, source, origin in ((0, tail_ref, 120), (1, head_ref, 0)):
        for group in range(2):
            packed = jnp.zeros((64, 128), F32)
            for k in range(16):
                value = source[group * 16 + k].astype(F32)
                shift = (8 * k - origin) % 128
                value = pltpu.roll(value, shift, 1) if shift else value
                packed = jnp.where((lane >= 8 * k) & (lane < 8 * k + 8), value, packed)
            packed_ref[which, group] = packed.astype(BF)
    for which, dy in ((0, 1), (1, -1)):
        send(
            0, dy, packed_ref.at[which], landed_ref.at[which],
            rim_send.at[6 + which], rim_recv.at[6 + which],
        )

    for dz, dy, copy in guarded:
        pl.when(exists(-dz, -dy))(copy.wait_recv)
    for copy in marks:
        copy.wait_recv()

    zero = jnp.zeros((64, 128), F32)
    for group in range(2):
        before = landed_ref[0, group].astype(F32)
        after = landed_ref[1, group].astype(F32)
        for k in range(16):
            up = (120 - 8 * k) % 128
            down = (-8 * k) % 128
            left = pltpu.roll(before, up, 1) if up else before
            right = pltpu.roll(after, down, 1) if down else after
            value = jnp.where(lane < 8, right, jnp.where(lane >= 120, left, zero))
            edge_ref[group * 16 + k] = value.astype(BF)
    for layer in range(2):
        left = corner_ref[2 * layer].astype(F32)
        right = corner_ref[2 * layer + 1].astype(F32)
        value = jnp.where(lane < 8, right, jnp.where(lane >= 120, left, zero))
        edge_ref[SIDE + layer] = value.astype(BF)

    for dz, dy, copy in guarded:
        pl.when(exists(dz, dy))(copy.wait_send)
    for copy in marks:
        copy.wait_send()


def exchange(volume, occupancy, slabs, groups, columns):
    vmem = pl.BlockSpec(memory_space=pltpu.VMEM)
    anywhere = pl.BlockSpec(memory_space=pl.ANY)
    dma = pltpu.SemaphoreType.DMA
    return pl.pallas_call(
        functools.partial(exchange_kernel, slabs=slabs, groups=groups, columns=columns),
        out_shape=(
            jax.ShapeDtypeStruct((2,) + volume.shape[1:], BF),
            jax.ShapeDtypeStruct((SIDE + 2, 64, 128), BF),
            jax.ShapeDtypeStruct((groups, 8, 128), jnp.int32),
            jax.ShapeDtypeStruct((3, 3, 8, 128), jnp.int32),
        ),
        in_specs=[anywhere, vmem],
        out_specs=(anywhere, vmem, vmem, vmem),
        scratch_shapes=[
            pltpu.VMEM((SIDE, 64, 128), BF),
            pltpu.VMEM((SIDE, 64, 128), BF),
            pltpu.VMEM((2, 2, 64, 128), BF),
            pltpu.VMEM((2, 2, 64, 128), BF),
            pltpu.VMEM((4, 64, 128), BF),
            pltpu.VMEM((8, 128), jnp.int32),
            dma((2,)), dma((groups,)), dma((groups,)), dma((8,)), dma((8,)), dma((8,)), dma((8,)),
        ],
        compiler_params=pltpu.CompilerParams(
            collective_id=0, has_side_effects=True, vmem_limit_bytes=56 * 1024 * 1024
        ),
        cost_estimate=pl.CostEstimate(flops=0, bytes_accessed=2_000_000, transcendentals=0),
    )(volume, occupancy)


def per_device(volume, occupancy, device_order, weight_one, bias_one, weight_two, bias_two):
    columns = occupancy.shape[1]
    slabs = lax.axis_size("gz")
    groups = lax.axis_size("xy")
    zhalo, edge, table, near = exchange(volume, occupancy, slabs, groups, columns)
    count, cols, slots, flags, owner, part, w1, b1, w2, b2 = plan(
        table, near, device_order, weight_one, bias_one, weight_two, bias_two, groups, columns
    )
    arrived = []
    earlier = ()
    for begin in range(0, columns, groups):
        made = compute_bricks(
            count, cols, slots, flags, volume, zhalo, edge, w1, b1, w2, b2, earlier,
            groups, columns, begin, min(groups, columns - begin),
        )
        earlier = (made,)
        arrived.append(
            lax.all_to_all(made, "xy", split_axis=0, concat_axis=0, tiled=True)
        )
    return collect(owner, part, arrived, columns // 2)


def solution(mesh):
    in_specs = (P("gz", None, "xy"), P("gz", "xy"), P("gz", None), P(), P(), P(), P())
    out_specs = P(("gz", "xy"), None, None)
    return jax.shard_map(
        per_device, mesh=mesh, in_specs=in_specs, out_specs=out_specs, check_vma=False
    )
```

```python
import functools

import numpy as np
import jax
import jax.numpy as jnp
from jax import lax
from jax.experimental import pallas as pl
from jax.experimental.pallas import tpu as pltpu
from jax.sharding import PartitionSpec as P

BF = jnp.bfloat16
F32 = jnp.float32
SIDE = 32
ACROSS = 4
PITCH = 40


def spread_matrix():
    table = np.zeros((ACROSS * PITCH, 256), np.float32)
    for x in range(ACROSS):
        for y in range(SIDE):
            table[x * PITCH + y + 2, y * ACROSS + x] = 1
        for y in range(2):
            table[x * PITCH + 34 + y, 128 + y * ACROSS + x] = 1
            table[x * PITCH + y, 128 + (30 + y) * ACROSS + x] = 1
    return table


def interleave_matrices():
    table = np.zeros((2, 256, 512), np.float32)
    for x in range(2):
        table[x, np.arange(256), np.arange(256) * 2 + x] = 1
    return table


def banded(taps):
    zero = jnp.zeros_like(taps[..., 0, :, :])
    rows = []
    for xi in range(ACROSS):
        blocks = []
        for xo in range(ACROSS):
            tap = xi - xo + 1
            blocks.append(taps[..., tap, :, :] if 0 <= tap < 3 else zero)
        rows.append(jnp.concatenate(blocks, axis=-1))
    return jnp.concatenate(rows, axis=-2)


def brick_kernel(
    n_ref, cols_ref, slots_ref, flags_ref,
    main_ref, prev_ref, next_ref, zmain_ref, zprev_ref, znext_ref, edge_ref,
    spread_ref, inter_ref, w1_ref, b1_ref, w2_ref, b2_ref, *refs,
    columns,
):
    out_ref, ext_ref, hid_ref, taps_ref, pool_ref = refs[-5:]
    step = pl.program_id(0)

    @pl.when(step < n_ref[0])
    def _():
        col = cols_ref[step]
        first = col == 0
        last = col == columns - 1

        def flag(a, b):
            return flags_ref[step * 9 + 3 * a + b].astype(F32)

        lane = lax.broadcasted_iota(jnp.int32, (1, 1, 128), 2)
        low = lane < 64
        from_edge = jnp.where(low, last.astype(jnp.int32), first.astype(jnp.int32)) > 0

        def keep(value, mark):
            return jnp.where(mark > 0, value, jnp.zeros((), BF))

        def rim(before, after, edge, a):
            value = jnp.where(from_edge, edge, jnp.where(low, after, before))
            return keep(value, jnp.where(low, flag(a, 2), flag(a, 0)))

        spread = spread_ref[...]

        def put(own, side, first_layer):
            count = own.shape[0]
            both = jnp.concatenate(
                [own.reshape(count * 64, 128), side.reshape(count * 64, 128)], axis=1
            )
            turned = lax.dot_general(
                spread, both, (((1,), (1,)), ((), ())), preferred_element_type=F32
            )
            for k in range(count):
                for half in range(2):
                    pieces = [
                        turned[x * PITCH:(x + 1) * PITCH, k * 64:(k + 1) * 64]
                        for x in (2 * half, 2 * half + 1)
                    ]
                    ext_ref[first_layer + k, 0:PITCH, half * 128:(half + 1) * 128] = (
                        jnp.concatenate(pieces, axis=1)
                    )

        def put_main(k):
            at = slice(4 * k, 4 * k + 4)
            put(main_ref[at], rim(prev_ref[at], next_ref[at], edge_ref[at], 1), 4 * k + 1)

        def put_rim(layer, a, spot):
            at = slice(layer, layer + 1)
            side = rim(zprev_ref[at], znext_ref[at], edge_ref[32 + layer:33 + layer], a)
            put(keep(zmain_ref[at], flag(a, 1)), side, spot)

        y_at = lax.broadcasted_iota(jnp.int32, (PITCH, 256), 0)
        regions = [
            jnp.where(y_at == 0, flag(a, 0), jnp.where(y_at == 33, flag(a, 2), flag(a, 1)))
            for a in range(3)
        ]
        bias_one = b1_ref[...]
        bias_two = b2_ref[...]

        def first_conv(z, count):
            rows = [
                ext_ref[z:z + count, t:t + PITCH, :].reshape(count * PITCH, 256).astype(BF)
                for t in range(3)
            ]
            total = jnp.dot(
                jnp.concatenate(rows, axis=1), w1_ref[...], preferred_element_type=F32
            )
            act = jnp.maximum(total + bias_one, 0.0).reshape(count, PITCH, 256)
            for k in range(count):
                zone = 0 if z + k == 0 else 2 if z + k == 33 else 1
                hid_ref[z + k] = act[k] * regions[zone]
            for t in range(3):
                taps_ref[z:z + count, :, t * 256:(t + 1) * 256] = hid_ref[
                    z:z + count, t:t + SIDE, :
                ].astype(BF)

        def second_conv(z):
            rows = [taps_ref[z + a:z + a + 8].reshape(8 * SIDE, 768) for a in range(3)]
            total = jnp.dot(
                jnp.concatenate(rows, axis=1), w2_ref[...], preferred_element_type=F32
            )
            act = jnp.maximum(total + bias_two, 0.0).reshape(4, 2, SIDE, 256)
            act = act[:, 0] + act[:, 1]
            left, right = act[..., :128], act[..., 128:]
            left = left + pltpu.roll(left, 64, 2)
            right = right + pltpu.roll(right, 64, 2)
            pool_ref[z // 2:z // 2 + 4] = jnp.where(low, left, right)

        put_rim(0, 0, 0)
        put_main(0)
        put_main(1)
        first_conv(0, 9)
        put_main(2)
        put_main(3)
        first_conv(9, 8)
        second_conv(0)
        put_main(4)
        put_main(5)
        first_conv(17, 8)
        second_conv(8)
        put_main(6)
        put_main(7)
        put_rim(1, 2, 33)
        first_conv(25, 9)
        second_conv(16)
        second_conv(24)
        pooled = pool_ref[:, pl.ds(0, 16, stride=2), :] + pool_ref[:, pl.ds(1, 16, stride=2), :]
        pooled = (pooled * 0.125).reshape(256, 128)
        turned = jnp.transpose(pooled).astype(BF)
        result = jnp.dot(turned[:64], inter_ref[0], preferred_element_type=F32)
        result = result + jnp.dot(turned[64:], inter_ref[1], preferred_element_type=F32)
        out_ref[0] = result.astype(BF)


def compute_bricks(
    count, cols, slots, flags, volume, zhalo, edge, w1, b1, w2, b2, earlier, out_slots, columns, steps
):
    spread = jnp.asarray(spread_matrix(), BF)
    inter = jnp.asarray(interleave_matrices(), BF)

    def at(shift):
        def index(i, n, c, s, f):
            return (0, 0, jnp.clip(c[i] + shift, 0, columns - 1))
        return index

    def whole(shape):
        return pl.BlockSpec(shape, lambda i, n, c, s, f: (0,) * len(shape))

    grid_spec = pltpu.PrefetchScalarGridSpec(
        num_scalar_prefetch=4,
        grid=(steps,),
        in_specs=[pl.BlockSpec((SIDE, 64, 128), at(s)) for s in (0, -1, 1)]
        + [pl.BlockSpec((2, 64, 128), at(s)) for s in (0, -1, 1)]
        + [whole(v.shape) for v in (edge, spread, inter, w1, b1, w2, b2)]
        + [pl.BlockSpec(memory_space=pl.ANY)] * len(earlier),
        out_specs=pl.BlockSpec((1, 64, 512), lambda i, n, c, s, f: (s[i], 0, 0)),
        scratch_shapes=[
            pltpu.VMEM((34, 48, 256), F32),
            pltpu.VMEM((34, PITCH, 256), F32),
            pltpu.VMEM((34, SIDE, 768), BF),
            pltpu.VMEM((16, SIDE, 128), F32),
        ],
    )
    return pl.pallas_call(
        functools.partial(brick_kernel, columns=columns),
        out_shape=jax.ShapeDtypeStruct((out_slots, 64, 512), BF),
        grid_spec=grid_spec,
        compiler_params=pltpu.CompilerParams(
            dimension_semantics=("arbitrary",), vmem_limit_bytes=48 * 1024 * 1024
        ),
        cost_estimate=pl.CostEstimate(
            flops=steps * 1_600_000_000, bytes_accessed=steps * 1_600_000, transcendentals=0
        ),
    )(count, cols, slots, flags, volume, volume, volume, zhalo, zhalo, zhalo, edge,
      spread, inter, w1, b1, w2, b2, *earlier)


MESH = pl.DeviceIdType.MESH


def exchange_kernel(
    volume_ref, occ_ref, zhalo_ref, edge_ref, table_ref, near_ref,
    head_ref, tail_ref, packed_ref, landed_ref, corner_ref, occ_out_ref,
    local_sem, occ_send, occ_recv, near_send, near_recv, rim_send, rim_recv,
    *, slabs, groups, columns,
):
    gz = lax.axis_index("gz")
    xy = lax.axis_index("xy")
    span = volume_ref.shape[2]

    def exists(dz, dy):
        return (gz + dz >= 0) & (gz + dz < slabs) & (xy + dy >= 0) & (xy + dy < groups)

    around = [(dz, dy) for dz in (-1, 0, 1) for dy in (-1, 0, 1) if (dz, dy) != (0, 0)]
    local = [
        pltpu.make_async_copy(volume_ref.at[:, :, pl.ds(0, 128)], head_ref, local_sem.at[0]),
        pltpu.make_async_copy(
            volume_ref.at[:, :, pl.ds(span - 128, 128)], tail_ref, local_sem.at[1]
        ),
    ]
    for copy in local:
        copy.start()

    occ_out_ref[...] = jnp.zeros((8, 128), jnp.int32)
    occ_out_ref[0:1, 0:columns] = occ_ref[...]
    near_ref[...] = jnp.zeros((3, 3, 8, 128), jnp.int32)
    near_ref[1, 1] = occ_out_ref[...]
    landed_ref[...] = jnp.zeros_like(landed_ref)
    corner_ref[...] = jnp.zeros_like(corner_ref)
    table_ref[xy] = occ_out_ref[...]

    barrier = pltpu.get_barrier_semaphore()
    partners = groups - 1
    for step in range(1, groups):
        pl.semaphore_signal(
            barrier, inc=1, device_id=(gz, lax.rem(xy + step, groups)), device_id_type=MESH
        )
    for dz, dy in around:
        if dz != 0:
            partners = partners + exists(dz, dy).astype(jnp.int32)

            @pl.when(exists(dz, dy))
            def _(dz=dz, dy=dy):
                pl.semaphore_signal(
                    barrier, inc=1, device_id=(gz + dz, xy + dy), device_id_type=MESH
                )

    pl.semaphore_wait(barrier, partners)

    marks = []
    for step in range(1, groups):
        marks.append(pltpu.make_async_remote_copy(
            src_ref=occ_out_ref, dst_ref=table_ref.at[xy],
            send_sem=occ_send.at[step], recv_sem=occ_recv.at[step],
            device_id=(gz, lax.rem(xy + step, groups)), device_id_type=MESH,
        ))
        marks[-1].start()

    guarded = []

    def send(dz, dy, src, dst, send_sem, recv_sem):
        copy = pltpu.make_async_remote_copy(
            src_ref=src, dst_ref=dst, send_sem=send_sem, recv_sem=recv_sem,
            device_id=(gz + dz, xy + dy), device_id_type=MESH,
        )
        pl.when(exists(dz, dy))(copy.start)
        guarded.append((dz, dy, copy))

    send(1, 0, volume_ref.at[SIDE - 1], zhalo_ref.at[0], rim_send.at[0], rim_recv.at[0])
    send(-1, 0, volume_ref.at[0], zhalo_ref.at[1], rim_send.at[1], rim_recv.at[1])
    for k, (dz, dy) in enumerate(around):
        send(
            dz, dy, occ_out_ref, near_ref.at[1 - dz, 1 - dy], near_send.at[k], near_recv.at[k]
        )
    for copy in local:
        copy.wait()
    corners = (
        (1, 1, tail_ref, SIDE - 1), (1, -1, head_ref, SIDE - 1),
        (-1, 1, tail_ref, 0), (-1, -1, head_ref, 0),
    )
    for k, (dz, dy, source, layer) in enumerate(corners):
        send(dz, dy, source.at[layer], corner_ref.at[k], rim_send.at[2 + k], rim_recv.at[2 + k])

    lane = lax.broadcasted_iota(jnp.int32, (1, 128), 1)
    for which, source, origin in ((0, tail_ref, 120), (1, head_ref, 0)):
        for group in range(2):
            packed = jnp.zeros((64, 128), F32)
            for k in range(16):
                value = source[group * 16 + k].astype(F32)
                shift = (8 * k - origin) % 128
                value = pltpu.roll(value, shift, 1) if shift else value
                packed = jnp.where((lane >= 8 * k) & (lane < 8 * k + 8), value, packed)
            packed_ref[which, group] = packed.astype(BF)
    for which, dy in ((0, 1), (1, -1)):
        send(
            0, dy, packed_ref.at[which], landed_ref.at[which],
            rim_send.at[6 + which], rim_recv.at[6 + which],
        )

    for dz, dy, copy in guarded:
        pl.when(exists(-dz, -dy))(copy.wait_recv)
    for copy in marks:
        copy.wait_recv()

    zero = jnp.zeros((64, 128), F32)
    for group in range(2):
        before = landed_ref[0, group].astype(F32)
        after = landed_ref[1, group].astype(F32)
        for k in range(16):
            up = (120 - 8 * k) % 128
            down = (-8 * k) % 128
            left = pltpu.roll(before, up, 1) if up else before
            right = pltpu.roll(after, down, 1) if down else after
            value = jnp.where(lane < 8, right, jnp.where(lane >= 120, left, zero))
            edge_ref[group * 16 + k] = value.astype(BF)
    for layer in range(2):
        left = corner_ref[2 * layer].astype(F32)
        right = corner_ref[2 * layer + 1].astype(F32)
        value = jnp.where(lane < 8, right, jnp.where(lane >= 120, left, zero))
        edge_ref[SIDE + layer] = value.astype(BF)

    for dz, dy, copy in guarded:
        pl.when(exists(dz, dy))(copy.wait_send)
    for copy in marks:
        copy.wait_send()


def exchange(volume, occupancy, slabs, groups, columns):
    vmem = pl.BlockSpec(memory_space=pltpu.VMEM)
    anywhere = pl.BlockSpec(memory_space=pl.ANY)
    dma = pltpu.SemaphoreType.DMA
    return pl.pallas_call(
        functools.partial(exchange_kernel, slabs=slabs, groups=groups, columns=columns),
        out_shape=(
            jax.ShapeDtypeStruct((2,) + volume.shape[1:], BF),
            jax.ShapeDtypeStruct((SIDE + 2, 64, 128), BF),
            jax.ShapeDtypeStruct((groups, 8, 128), jnp.int32),
            jax.ShapeDtypeStruct((3, 3, 8, 128), jnp.int32),
        ),
        in_specs=[anywhere, vmem],
        out_specs=(anywhere, vmem, vmem, vmem),
        scratch_shapes=[
            pltpu.VMEM((SIDE, 64, 128), BF),
            pltpu.VMEM((SIDE, 64, 128), BF),
            pltpu.VMEM((2, 2, 64, 128), BF),
            pltpu.VMEM((2, 2, 64, 128), BF),
            pltpu.VMEM((4, 64, 128), BF),
            pltpu.VMEM((8, 128), jnp.int32),
            dma((2,)), dma((groups,)), dma((groups,)), dma((8,)), dma((8,)), dma((8,)), dma((8,)),
        ],
        compiler_params=pltpu.CompilerParams(
            collective_id=0, has_side_effects=True, vmem_limit_bytes=16 * 1024 * 1024
        ),
        cost_estimate=pl.CostEstimate(flops=0, bytes_accessed=2_000_000, transcendentals=0),
    )(volume, occupancy)


def per_device(volume, occupancy, device_order, weight_one, bias_one, weight_two, bias_two):
    columns = occupancy.shape[1]
    slabs = lax.axis_size("gz")
    groups = lax.axis_size("xy")
    slot_count = columns // 2
    me = lax.axis_index("xy")
    zhalo, edge, table, near = exchange(volume, occupancy, slabs, groups, columns)
    total = groups * columns
    row = table[:, 0, :columns].reshape(total)
    near = near[:, :, 0, :columns].reshape(3, 3 * columns)[:, columns - 1:2 * columns + 1]
    own = occupancy[0]
    order = device_order[0]
    ids = jnp.arange(columns, dtype=jnp.int32)
    labels = jnp.arange(groups, dtype=jnp.int32)
    everyone = jnp.arange(total, dtype=jnp.int32)
    local_rank = jnp.sum(jnp.where(ids[None, :] < ids[:, None], own[None, :], 0), axis=1)
    start = jnp.sum(jnp.where(everyone < me * columns, row, 0))
    label = (start + local_rank) % groups
    target = jnp.sum(jnp.where(label[:, None] == labels[None, :], order[None, :], 0), axis=1)
    count = jnp.sum(own)
    flag_of = jnp.stack([near[a, b:b + columns] for a in range(3) for b in range(3)], axis=1)
    early = columns - groups

    def part(begin, end):
        amount = jnp.clip(count - begin, 0, end - begin)
        wanted = begin + jnp.minimum(
            jnp.arange(end - begin, dtype=jnp.int32), jnp.maximum(amount - 1, 0)
        )
        hit = (local_rank[None, :] == wanted[:, None]) & (own[None, :] > 0)
        cols = jnp.sum(jnp.where(hit, ids[None, :], 0), axis=1)
        part_capacity = (end - begin + groups - 1) // groups
        slot = target * part_capacity + (local_rank - begin) // groups
        slots = jnp.sum(jnp.where(hit, slot[None, :], 0), axis=1)
        flags = jnp.sum(jnp.where(hit[:, :, None], flag_of[None], 0), axis=1).reshape(-1)
        return amount.reshape(1), cols, slots, flags, part_capacity

    w1 = banded(weight_one.reshape(64, 3, 3, 64).transpose(1, 2, 3, 0)).reshape(768, 256)
    w2 = banded(weight_two.reshape(64, 3, 3, 3, 64).transpose(1, 2, 3, 4, 0)).reshape(2304, 256)
    b1 = jnp.tile(bias_one, ACROSS)[None]
    b2 = jnp.tile(bias_two, ACROSS)[None]

    arrived = []
    earlier = ()
    for begin, end in ((0, early), (early, columns)):
        if begin < end:
            amount, cols, slots, flags, part_capacity = part(begin, end)
            made = compute_bricks(
                amount, cols, slots, flags, volume, zhalo, edge, w1, b1, w2, b2,
                earlier, groups * part_capacity, columns, end - begin,
            )
            earlier = (made,)
            sent = lax.all_to_all(made, "xy", split_axis=0, concat_axis=0, tiled=True)
            arrived.append(sent.reshape(groups, part_capacity, 64, 512))
    arrived = jnp.concatenate(arrived, axis=1).reshape(-1, 64, 512)

    my_label = jnp.sum(jnp.where(order == me, labels, 0))
    need = jnp.arange(slot_count, dtype=jnp.int32) * groups + my_label
    counts = row.reshape(groups, columns).sum(axis=1)
    starts = jnp.sum(jnp.where(labels[None, :] < labels[:, None], counts[None, :], 0), axis=1)
    owner = jnp.sum(((starts + counts)[None, :] <= need[:, None]).astype(jnp.int32), axis=1)
    owner_start = jnp.sum(jnp.where(labels[None, :] == owner[:, None], starts[None, :], 0), axis=1)
    rank = need - owner_start
    early_rows = (early + groups - 1) // groups
    place = jnp.where(rank < early, rank // groups, early_rows + (rank - early) // groups)
    return jnp.take(arrived, owner * (early_rows + 1) + place, axis=0, mode="clip")


def solution(mesh):
    in_specs = (P("gz", None, "xy"), P("gz", "xy"), P("gz", None), P(), P(), P(), P())
    out_specs = P(("gz", "xy"), None, None)
    return jax.shard_map(
        per_device, mesh=mesh, in_specs=in_specs, out_specs=out_specs, check_vma=False
    )
```

```python
import functools

import numpy as np
import jax
import jax.numpy as jnp
from jax import lax
from jax.experimental import pallas as pl
from jax.experimental.pallas import tpu as pltpu
from jax.sharding import PartitionSpec as P

BF = jnp.bfloat16
F32 = jnp.float32
SIDE = 32
ACROSS = 4
PITCH = 40


def spread_matrix():
    table = np.zeros((ACROSS * PITCH, 256), np.float32)
    for x in range(ACROSS):
        for y in range(SIDE):
            table[x * PITCH + y + 2, y * ACROSS + x] = 1
        for y in range(2):
            table[x * PITCH + 34 + y, 128 + y * ACROSS + x] = 1
            table[x * PITCH + y, 128 + (30 + y) * ACROSS + x] = 1
    return table


def interleave_matrices():
    table = np.zeros((2, 256, 512), np.float32)
    for x in range(2):
        table[x, np.arange(256), np.arange(256) * 2 + x] = 1
    return table


def banded(taps):
    zero = jnp.zeros_like(taps[..., 0, :, :])
    rows = []
    for xi in range(ACROSS):
        blocks = []
        for xo in range(ACROSS):
            tap = xi - xo + 1
            blocks.append(taps[..., tap, :, :] if 0 <= tap < 3 else zero)
        rows.append(jnp.concatenate(blocks, axis=-1))
    return jnp.concatenate(rows, axis=-2)


def brick_kernel(
    n_ref, cols_ref, slots_ref, flags_ref,
    main_ref, prev_ref, next_ref, zmain_ref, zprev_ref, znext_ref, edge_ref,
    spread_ref, inter_ref, w1_ref, b1_ref, w2_ref, b2_ref,
    out_ref,
    ext_ref, hid_ref, taps_ref, pool_ref,
    *, columns,
):
    step = pl.program_id(0)

    @pl.when(step < n_ref[0])
    def _():
        col = cols_ref[step]
        first = col == 0
        last = col == columns - 1

        def flag(a, b):
            return flags_ref[step * 9 + 3 * a + b].astype(F32)

        lane = lax.broadcasted_iota(jnp.int32, (1, 1, 128), 2)
        low = lane < 64
        from_edge = jnp.where(low, last.astype(jnp.int32), first.astype(jnp.int32)) > 0

        def keep(value, mark):
            return jnp.where(mark > 0, value, jnp.zeros((), BF))

        def rim(before, after, edge, a):
            value = jnp.where(from_edge, edge, jnp.where(low, after, before))
            return keep(value, jnp.where(low, flag(a, 2), flag(a, 0)))

        spread = spread_ref[...]

        def put(own, side, first_layer):
            count = own.shape[0]
            both = jnp.concatenate(
                [own.reshape(count * 64, 128), side.reshape(count * 64, 128)], axis=1
            )
            turned = lax.dot_general(
                spread, both, (((1,), (1,)), ((), ())), preferred_element_type=F32
            )
            for k in range(count):
                for half in range(2):
                    pieces = [
                        turned[x * PITCH:(x + 1) * PITCH, k * 64:(k + 1) * 64]
                        for x in (2 * half, 2 * half + 1)
                    ]
                    ext_ref[first_layer + k, 0:PITCH, half * 128:(half + 1) * 128] = (
                        jnp.concatenate(pieces, axis=1)
                    )

        def put_main(k):
            at = slice(4 * k, 4 * k + 4)
            put(main_ref[at], rim(prev_ref[at], next_ref[at], edge_ref[at], 1), 4 * k + 1)

        def put_rim(layer, a, spot):
            at = slice(layer, layer + 1)
            side = rim(zprev_ref[at], znext_ref[at], edge_ref[32 + layer:33 + layer], a)
            put(keep(zmain_ref[at], flag(a, 1)), side, spot)

        y_at = lax.broadcasted_iota(jnp.int32, (PITCH, 256), 0)
        regions = [
            jnp.where(y_at == 0, flag(a, 0), jnp.where(y_at == 33, flag(a, 2), flag(a, 1)))
            for a in range(3)
        ]
        bias_one = b1_ref[...]
        bias_two = b2_ref[...]

        def first_conv(z, count):
            rows = [
                ext_ref[z:z + count, t:t + PITCH, :].reshape(count * PITCH, 256).astype(BF)
                for t in range(3)
            ]
            total = jnp.dot(
                jnp.concatenate(rows, axis=1), w1_ref[...], preferred_element_type=F32
            )
            act = jnp.maximum(total + bias_one, 0.0).reshape(count, PITCH, 256)
            for k in range(count):
                zone = 0 if z + k == 0 else 2 if z + k == 33 else 1
                hid_ref[z + k] = act[k] * regions[zone]
            for t in range(3):
                taps_ref[z:z + count, :, t * 256:(t + 1) * 256] = hid_ref[
                    z:z + count, t:t + SIDE, :
                ].astype(BF)

        def second_conv(z):
            rows = [taps_ref[z + a:z + a + 8].reshape(8 * SIDE, 768) for a in range(3)]
            total = jnp.dot(
                jnp.concatenate(rows, axis=1), w2_ref[...], preferred_element_type=F32
            )
            act = jnp.maximum(total + bias_two, 0.0).reshape(4, 2, SIDE, 256)
            act = act[:, 0] + act[:, 1]
            left, right = act[..., :128], act[..., 128:]
            left = left + pltpu.roll(left, 64, 2)
            right = right + pltpu.roll(right, 64, 2)
            pool_ref[z // 2:z // 2 + 4] = jnp.where(low, left, right)

        put_rim(0, 0, 0)
        put_main(0)
        put_main(1)
        first_conv(0, 9)
        put_main(2)
        put_main(3)
        first_conv(9, 8)
        second_conv(0)
        put_main(4)
        put_main(5)
        first_conv(17, 8)
        second_conv(8)
        put_main(6)
        put_main(7)
        put_rim(1, 2, 33)
        first_conv(25, 9)
        second_conv(16)
        second_conv(24)
        pooled = pool_ref[:, pl.ds(0, 16, stride=2), :] + pool_ref[:, pl.ds(1, 16, stride=2), :]
        pooled = (pooled * 0.125).reshape(256, 128)
        turned = jnp.transpose(pooled).astype(BF)
        result = jnp.dot(turned[:64], inter_ref[0], preferred_element_type=F32)
        result = result + jnp.dot(turned[64:], inter_ref[1], preferred_element_type=F32)
        out_ref[0] = result.astype(BF)


def compute_bricks(
    count, cols, slots, flags, volume, zhalo, edge, w1, b1, w2, b2, out_slots, columns, steps
):
    spread = jnp.asarray(spread_matrix(), BF)
    inter = jnp.asarray(interleave_matrices(), BF)

    def at(shift):
        def index(i, n, c, s, f):
            return (0, 0, jnp.clip(c[i] + shift, 0, columns - 1))
        return index

    def whole(shape):
        return pl.BlockSpec(shape, lambda i, n, c, s, f: (0,) * len(shape))

    grid_spec = pltpu.PrefetchScalarGridSpec(
        num_scalar_prefetch=4,
        grid=(steps,),
        in_specs=[pl.BlockSpec((SIDE, 64, 128), at(s)) for s in (0, -1, 1)]
        + [pl.BlockSpec((2, 64, 128), at(s)) for s in (0, -1, 1)]
        + [whole(v.shape) for v in (edge, spread, inter, w1, b1, w2, b2)],
        out_specs=pl.BlockSpec((1, 64, 512), lambda i, n, c, s, f: (s[i], 0, 0)),
        scratch_shapes=[
            pltpu.VMEM((34, 48, 256), F32),
            pltpu.VMEM((34, PITCH, 256), F32),
            pltpu.VMEM((34, SIDE, 768), BF),
            pltpu.VMEM((16, SIDE, 128), F32),
        ],
    )
    return pl.pallas_call(
        functools.partial(brick_kernel, columns=columns),
        out_shape=jax.ShapeDtypeStruct((out_slots, 64, 512), BF),
        grid_spec=grid_spec,
        compiler_params=pltpu.CompilerParams(
            dimension_semantics=("arbitrary",), vmem_limit_bytes=48 * 1024 * 1024
        ),
        cost_estimate=pl.CostEstimate(
            flops=steps * 1_600_000_000, bytes_accessed=steps * 1_600_000, transcendentals=0
        ),
    )(count, cols, slots, flags, volume, volume, volume, zhalo, zhalo, zhalo, edge,
      spread, inter, w1, b1, w2, b2)


MESH = pl.DeviceIdType.MESH


def exchange_kernel(
    volume_ref, occ_ref, zhalo_ref, edge_ref, table_ref, near_ref,
    head_ref, tail_ref, packed_ref, landed_ref, corner_ref, occ_out_ref,
    local_sem, occ_send, occ_recv, near_send, near_recv, rim_send, rim_recv,
    *, slabs, groups, columns,
):
    gz = lax.axis_index("gz")
    xy = lax.axis_index("xy")
    span = volume_ref.shape[2]

    def exists(dz, dy):
        return (gz + dz >= 0) & (gz + dz < slabs) & (xy + dy >= 0) & (xy + dy < groups)

    around = [(dz, dy) for dz in (-1, 0, 1) for dy in (-1, 0, 1) if (dz, dy) != (0, 0)]
    local = [
        pltpu.make_async_copy(volume_ref.at[:, :, pl.ds(0, 128)], head_ref, local_sem.at[0]),
        pltpu.make_async_copy(
            volume_ref.at[:, :, pl.ds(span - 128, 128)], tail_ref, local_sem.at[1]
        ),
    ]
    for copy in local:
        copy.start()

    occ_out_ref[...] = jnp.zeros((8, 128), jnp.int32)
    occ_out_ref[0:1, 0:columns] = occ_ref[...]
    near_ref[...] = jnp.zeros((3, 3, 8, 128), jnp.int32)
    near_ref[1, 1] = occ_out_ref[...]
    landed_ref[...] = jnp.zeros_like(landed_ref)
    corner_ref[...] = jnp.zeros_like(corner_ref)
    table_ref[xy] = occ_out_ref[...]

    barrier = pltpu.get_barrier_semaphore()
    partners = groups - 1
    for step in range(1, groups):
        pl.semaphore_signal(
            barrier, inc=1, device_id=(gz, lax.rem(xy + step, groups)), device_id_type=MESH
        )
    for dz, dy in around:
        if dz != 0:
            partners = partners + exists(dz, dy).astype(jnp.int32)

            @pl.when(exists(dz, dy))
            def _(dz=dz, dy=dy):
                pl.semaphore_signal(
                    barrier, inc=1, device_id=(gz + dz, xy + dy), device_id_type=MESH
                )

    pl.semaphore_wait(barrier, partners)

    marks = []
    for step in range(1, groups):
        marks.append(pltpu.make_async_remote_copy(
            src_ref=occ_out_ref, dst_ref=table_ref.at[xy],
            send_sem=occ_send.at[step], recv_sem=occ_recv.at[step],
            device_id=(gz, lax.rem(xy + step, groups)), device_id_type=MESH,
        ))
        marks[-1].start()

    guarded = []

    def send(dz, dy, src, dst, send_sem, recv_sem):
        copy = pltpu.make_async_remote_copy(
            src_ref=src, dst_ref=dst, send_sem=send_sem, recv_sem=recv_sem,
            device_id=(gz + dz, xy + dy), device_id_type=MESH,
        )
        pl.when(exists(dz, dy))(copy.start)
        guarded.append((dz, dy, copy))

    send(1, 0, volume_ref.at[SIDE - 1], zhalo_ref.at[0], rim_send.at[0], rim_recv.at[0])
    send(-1, 0, volume_ref.at[0], zhalo_ref.at[1], rim_send.at[1], rim_recv.at[1])
    for k, (dz, dy) in enumerate(around):
        send(
            dz, dy, occ_out_ref, near_ref.at[1 - dz, 1 - dy], near_send.at[k], near_recv.at[k]
        )
    for copy in local:
        copy.wait()
    corners = (
        (1, 1, tail_ref, SIDE - 1), (1, -1, head_ref, SIDE - 1),
        (-1, 1, tail_ref, 0), (-1, -1, head_ref, 0),
    )
    for k, (dz, dy, source, layer) in enumerate(corners):
        send(dz, dy, source.at[layer], corner_ref.at[k], rim_send.at[2 + k], rim_recv.at[2 + k])

    lane = lax.broadcasted_iota(jnp.int32, (1, 128), 1)
    for which, source, origin in ((0, tail_ref, 120), (1, head_ref, 0)):
        for group in range(2):
            packed = jnp.zeros((64, 128), F32)
            for k in range(16):
                value = source[group * 16 + k].astype(F32)
                shift = (8 * k - origin) % 128
                value = pltpu.roll(value, shift, 1) if shift else value
                packed = jnp.where((lane >= 8 * k) & (lane < 8 * k + 8), value, packed)
            packed_ref[which, group] = packed.astype(BF)
    for which, dy in ((0, 1), (1, -1)):
        send(
            0, dy, packed_ref.at[which], landed_ref.at[which],
            rim_send.at[6 + which], rim_recv.at[6 + which],
        )

    for dz, dy, copy in guarded:
        pl.when(exists(-dz, -dy))(copy.wait_recv)
    for copy in marks:
        copy.wait_recv()

    zero = jnp.zeros((64, 128), F32)
    for group in range(2):
        before = landed_ref[0, group].astype(F32)
        after = landed_ref[1, group].astype(F32)
        for k in range(16):
            up = (120 - 8 * k) % 128
            down = (-8 * k) % 128
            left = pltpu.roll(before, up, 1) if up else before
            right = pltpu.roll(after, down, 1) if down else after
            value = jnp.where(lane < 8, right, jnp.where(lane >= 120, left, zero))
            edge_ref[group * 16 + k] = value.astype(BF)
    for layer in range(2):
        left = corner_ref[2 * layer].astype(F32)
        right = corner_ref[2 * layer + 1].astype(F32)
        value = jnp.where(lane < 8, right, jnp.where(lane >= 120, left, zero))
        edge_ref[SIDE + layer] = value.astype(BF)

    for dz, dy, copy in guarded:
        pl.when(exists(dz, dy))(copy.wait_send)
    for copy in marks:
        copy.wait_send()


def exchange(volume, occupancy, slabs, groups, columns):
    vmem = pl.BlockSpec(memory_space=pltpu.VMEM)
    anywhere = pl.BlockSpec(memory_space=pl.ANY)
    dma = pltpu.SemaphoreType.DMA
    return pl.pallas_call(
        functools.partial(exchange_kernel, slabs=slabs, groups=groups, columns=columns),
        out_shape=(
            jax.ShapeDtypeStruct((2,) + volume.shape[1:], BF),
            jax.ShapeDtypeStruct((SIDE + 2, 64, 128), BF),
            jax.ShapeDtypeStruct((groups, 8, 128), jnp.int32),
            jax.ShapeDtypeStruct((3, 3, 8, 128), jnp.int32),
        ),
        in_specs=[anywhere, vmem],
        out_specs=(anywhere, vmem, vmem, vmem),
        scratch_shapes=[
            pltpu.VMEM((SIDE, 64, 128), BF),
            pltpu.VMEM((SIDE, 64, 128), BF),
            pltpu.VMEM((2, 2, 64, 128), BF),
            pltpu.VMEM((2, 2, 64, 128), BF),
            pltpu.VMEM((4, 64, 128), BF),
            pltpu.VMEM((8, 128), jnp.int32),
            dma((2,)), dma((groups,)), dma((groups,)), dma((8,)), dma((8,)), dma((8,)), dma((8,)),
        ],
        compiler_params=pltpu.CompilerParams(
            collective_id=0, has_side_effects=True, vmem_limit_bytes=16 * 1024 * 1024
        ),
        cost_estimate=pl.CostEstimate(flops=0, bytes_accessed=2_000_000, transcendentals=0),
    )(volume, occupancy)


def per_device(volume, occupancy, device_order, weight_one, bias_one, weight_two, bias_two):
    columns = occupancy.shape[1]
    slabs = lax.axis_size("gz")
    groups = lax.axis_size("xy")
    capacity = (columns + groups - 1) // groups
    slot_count = columns // 2
    me = lax.axis_index("xy")
    zhalo, edge, table, near = exchange(volume, occupancy, slabs, groups, columns)
    total = groups * columns
    row = table[:, 0, :columns].reshape(total)
    near = near[:, :, 0, :columns].reshape(3, 3 * columns)[:, columns - 1:2 * columns + 1]
    own = occupancy[0]
    order = device_order[0]
    ids = jnp.arange(columns, dtype=jnp.int32)
    labels = jnp.arange(groups, dtype=jnp.int32)
    everyone = jnp.arange(total, dtype=jnp.int32)
    local_rank = jnp.sum(jnp.where(ids[None, :] < ids[:, None], own[None, :], 0), axis=1)
    start = jnp.sum(jnp.where(everyone < me * columns, row, 0))
    label = (start + local_rank) % groups
    target = jnp.sum(jnp.where(label[:, None] == labels[None, :], order[None, :], 0), axis=1)
    count = jnp.sum(own)
    flag_of = jnp.stack([near[a, b:b + columns] for a in range(3) for b in range(3)], axis=1)
    early = min(columns, 2 * groups)

    def part(begin, end):
        amount = jnp.clip(count - begin, 0, end - begin)
        wanted = begin + jnp.minimum(
            jnp.arange(end - begin, dtype=jnp.int32), jnp.maximum(amount - 1, 0)
        )
        hit = (local_rank[None, :] == wanted[:, None]) & (own[None, :] > 0)
        cols = jnp.sum(jnp.where(hit, ids[None, :], 0), axis=1)
        part_capacity = (end - begin + groups - 1) // groups
        slot = target * part_capacity + (local_rank - begin) // groups
        slots = jnp.sum(jnp.where(hit, slot[None, :], 0), axis=1)
        flags = jnp.sum(jnp.where(hit[:, :, None], flag_of[None], 0), axis=1).reshape(-1)
        return amount.reshape(1), cols, slots, flags, part_capacity

    w1 = banded(weight_one.reshape(64, 3, 3, 64).transpose(1, 2, 3, 0)).reshape(768, 256)
    w2 = banded(weight_two.reshape(64, 3, 3, 3, 64).transpose(1, 2, 3, 4, 0)).reshape(2304, 256)
    b1 = jnp.tile(bias_one, ACROSS)[None]
    b2 = jnp.tile(bias_two, ACROSS)[None]

    arrived = []
    for begin, end in ((0, early), (early, columns)):
        if begin < end:
            amount, cols, slots, flags, part_capacity = part(begin, end)
            made = compute_bricks(
                amount, cols, slots, flags, volume, zhalo, edge, w1, b1, w2, b2,
                groups * part_capacity, columns, end - begin,
            )
            sent = lax.all_to_all(made, "xy", split_axis=0, concat_axis=0, tiled=True)
            arrived.append(sent.reshape(groups, part_capacity, 64, 512))
    arrived = jnp.concatenate(arrived, axis=1).reshape(groups * capacity, 64, 512)

    my_label = jnp.sum(jnp.where(order == me, labels, 0))
    need = jnp.arange(slot_count, dtype=jnp.int32) * groups + my_label
    counts = row.reshape(groups, columns).sum(axis=1)
    starts = jnp.sum(jnp.where(labels[None, :] < labels[:, None], counts[None, :], 0), axis=1)
    owner = jnp.sum(((starts + counts)[None, :] <= need[:, None]).astype(jnp.int32), axis=1)
    owner_start = jnp.sum(jnp.where(labels[None, :] == owner[:, None], starts[None, :], 0), axis=1)
    arrival = owner * capacity + (need - owner_start) // groups
    return jnp.take(arrived, arrival, axis=0, mode="clip")


def solution(mesh):
    in_specs = (P("gz", None, "xy"), P("gz", "xy"), P("gz", None), P(), P(), P(), P())
    out_specs = P(("gz", "xy"), None, None)
    return jax.shard_map(
        per_device, mesh=mesh, in_specs=in_specs, out_specs=out_specs, check_vma=False
    )
```
